32 devices in a mesh: batch: 4 (over y, x), tok: 8 (over z, core).
Axes of the slice: x: 2, y: 2, z: 4, core: 2. Of those that a mesh axis runs over, the one named last changes fastest.
Arguments:
- inner_first: bfloat16 [512, 2048], P(('batch', 'tok')), parts along dimension 0, may hold values from -6 to 6
- gate_first: bfloat16 [512, 2048], P(('batch', 'tok')), parts along dimension 0, may hold values from -6 to 6
- bc_first: bfloat16 [512, 256], P(('batch', 'tok')), parts along dimension 0, may hold values from -4 to 4
- first_raw_steps: float32 [512, 32], P(('batch', 'tok')), parts along dimension 0
- rate_first: float32 [32], replicated, may hold values from 0 to 4
- bias_first: float32 [32], replicated, may hold values from -9 to -2.5
- skip_first: float32 [32], replicated, may hold values from 0.5 to 1.5
- norm_gain: float32 [2048], replicated, may hold values from 0.25 to 1.75
- out_weight: bfloat16 [2048, 2048], P('tok'), may hold values from -0.125 to 0.125
- residual: bfloat16 [512, 2048], P(('batch', 'tok')), parts along dimension 0, may hold values from -6 to 6
- pre_gain: float32 [2048], replicated, may hold values from 0.25 to 1.75
- in_weight: bfloat16 [2048, 2304], P('tok'), may hold values from -0.125 to 0.125
- conv_weight: bfloat16 [4, 2304], replicated, may hold values from -3 to 3
- conv_bias: float32 [2304], replicated, may hold values from -3 to 3
- step_weight: bfloat16 [2048, 32], replicated, may hold values from -0.0625 to 0.0625
- bias_second: float32 [32], replicated, may hold values from -9 to -2.5
- rate_second: float32 [32], replicated, may hold values from 0 to 4
- skip_second: float32 [32], replicated, may hold values from 0.5 to 1.5
- final_gain: float32 [2048], replicated, may hold values from 0.25 to 1.75
Outputs:
- mixed: bfloat16 [512, 2048], P(('batch', 'tok')), parts along dimension 0
The draws below stay inside these ranges and needn't reach their ends.
There are 4 independent parts, one for each index of `batch`. The reference program is written for one: setup_inputs(seed, part) draws one part's arguments, and reference() takes and returns one part's arrays. A program takes and returns all parts, laid end to end along the dimension named above; an argument that names none is the same for every part. Nothing has to cross between parts.
All inputs are finite; a program needn't handle non-finite values.
Results may differ from the reference program's by a relative error of at most 0.0075.
Values may be sent and summed in bfloat16 or wider, within the bound.
A program may use at most 192 MiB of HBM per device.

```python
import jax
import jax.numpy as jnp
from jax import lax

D = 2048
HEADS = 32
HEAD_SIZE = 64
STATE = 128
KC = 4
INNER = 2048
GRID_ROWS = 16
GRID_COLS = 8
TOK_DEV = 16
SAMPLE_TOKENS = 128
GROUP = 16


def head_law(key, salt, fast_share):
    key = jax.random.fold_in(key, salt)
    pick_key, short_key, long_key, factor_key = jax.random.split(key, 4)
    fast = jax.random.randint(pick_key, (HEADS,), 0, 1000) < int(1000 * fast_share)
    short_window = jax.random.uniform(short_key, (HEADS,), jnp.float32, 30.0, 50.0)
    long_window = SAMPLE_TOKENS * jnp.exp(jax.random.uniform(long_key, (HEADS,), jnp.float32, jnp.log(0.5), jnp.log(4.0)))
    window = jnp.where(fast, short_window, long_window)
    factor = jnp.exp(jax.random.uniform(factor_key, (HEADS,), jnp.float32, jnp.log(0.5), jnp.log(2.0)))
    return (window, 0.125 * factor / jnp.sqrt(window))


def group_rows(key):
    spots = jax.random.randint(jax.random.fold_in(key, 201), (3,), 0, SAMPLE_TOKENS)
    return jnp.any(jnp.arange(SAMPLE_TOKENS)[:, None] == spots[None, :], axis=1)


def draw_rate_first(key, part):
    share = 0.5
    window, typical = head_law(key, 101, share)
    return 1.0 / (typical * window)


def draw_bias_first(key, part):
    share = 0.5
    window, typical = head_law(key, 101, share)
    return jnp.log(jnp.expm1(typical))


def draw_rate_second(key, part):
    share = 0.5
    window, typical = head_law(key, 102, share)
    return 1.0 / (typical * window)


def draw_bias_second(key, part):
    share = 0.5
    window, typical = head_law(key, 102, share)
    return jnp.log(jnp.expm1(typical))


def draw_first_raw_steps(key, part):
    row_groups = group_rows(key)
    key = jax.random.fold_in(key, 301)
    noise_key, shift_key = jax.random.split(key)
    noise = 0.35 * jax.random.truncated_normal(noise_key, -3.0, 3.0, (SAMPLE_TOKENS, HEADS), jnp.float32)
    offsets = jnp.repeat(jax.random.uniform(shift_key, (SAMPLE_TOKENS // TOK_DEV,), jnp.float32, -0.7, 0.7), TOK_DEV)
    raise_amount = jnp.where(row_groups, jnp.log(0.8 * SAMPLE_TOKENS), 0.0)
    return noise + offsets[:, None] + raise_amount[:, None]


def draw_bc_first(key, part):
    row_groups = group_rows(key)
    key = jax.random.fold_in(key, 302)
    entries = jax.random.truncated_normal(key, -4.0, 4.0, (SAMPLE_TOKENS, 2 * STATE), jnp.float32)
    write_columns = jnp.arange(2 * STATE) < STATE
    decay_factor = jnp.where(row_groups[:, None] & write_columns[None, :], 1.0 / (0.8 * SAMPLE_TOKENS), 1.0)
    return (entries * decay_factor).astype(jnp.bfloat16)


def levels(stream_key, extent, shards, smallest, largest):
    factor_of, own = 1.0, jax.random.fold_in(stream_key, 6)
    for position, parts in shards:
        draws = jnp.exp(jax.random.uniform(jax.random.fold_in(own, position), (parts,), jnp.float32, smallest / len(shards), largest / len(shards)))
        factor_of = factor_of * jnp.repeat(draws, extent[position] // parts).reshape([-1 if axis == position else 1 for axis in range(len(extent))])
    return factor_of


def normal_values(key, shape, spread, limit, pieces=(), dtype=jnp.bfloat16):
    values = spread * jax.random.normal(key, shape, jnp.float32)
    if pieces:
        values = values * levels(key, shape, pieces, -0.22, 0.18)
    return jnp.clip(values, -limit, limit).astype(dtype)


def setup_inputs(seed: int = 0, part: int = 0) -> dict:
    splits = jax.random.split(jax.random.key(seed), 20)
    own_keys = jax.random.split(jax.random.fold_in(splits[19], part), 20)
    return {
        "inner_first": normal_values(own_keys[0], (SAMPLE_TOKENS, INNER), 1.0, 6.0, ((0, 8),)),
        "gate_first": normal_values(own_keys[1], (SAMPLE_TOKENS, INNER), 1.0, 6.0, ((0, 8),)),
        "bc_first": draw_bc_first(jax.random.fold_in(jax.random.fold_in(splits[19], part), 71), part),
        "first_raw_steps": draw_first_raw_steps(jax.random.fold_in(jax.random.fold_in(splits[19], part), 71), part),
        "rate_first": draw_rate_first(jax.random.fold_in(splits[19], 71), part),
        "bias_first": draw_bias_first(jax.random.fold_in(splits[19], 71), part),
        "skip_first": jnp.clip(jax.random.uniform(splits[6], (HEADS,), jnp.float32, 0.5, 1.5), 0.5, 1.5),
        "norm_gain": jnp.clip(1.0 + 0.15 * jax.random.normal(splits[7], (INNER,), jnp.float32), 0.25, 1.75),
        "out_weight": normal_values(splits[8], (INNER, D), INNER ** -0.5, 0.125, ((0, 8),)),
        "residual": normal_values(own_keys[9], (SAMPLE_TOKENS, D), 1.0, 6.0, ((0, 8),)),
        "pre_gain": jnp.clip(1.0 + 0.15 * jax.random.normal(splits[10], (D,), jnp.float32), 0.25, 1.75),
        "in_weight": normal_values(splits[11], (D, INNER + 2 * STATE), D ** -0.5, 0.125, ((0, 8),)),
        "conv_weight": normal_values(splits[12], (KC, INNER + 2 * STATE), KC ** -0.5, 3.0),
        "conv_bias": normal_values(splits[13], (INNER + 2 * STATE,), 0.5, 3.0, (), jnp.float32),
        "step_weight": normal_values(splits[14], (D, HEADS), (4 * D) ** -0.5, 0.0625),
        "bias_second": draw_bias_second(jax.random.fold_in(splits[19], 71), part),
        "rate_second": draw_rate_second(jax.random.fold_in(splits[19], 71), part),
        "skip_second": jnp.clip(jax.random.uniform(splits[17], (HEADS,), jnp.float32, 0.5, 1.5), 0.5, 1.5),
        "final_gain": jnp.clip(1.0 + 0.15 * jax.random.normal(splits[18], (INNER,), jnp.float32), 0.25, 1.75),
    }


def ssd(values, write_side, read_side, steps, rates, skips):
    total_rows = values.shape[0]
    blocks = total_rows // GROUP
    value_blocks = values.reshape(blocks, GROUP, HEADS, HEAD_SIZE)
    write_blocks = write_side.reshape(blocks, GROUP, STATE)
    read_blocks = read_side.reshape(blocks, GROUP, STATE)
    step_blocks = steps.reshape(blocks, GROUP, HEADS)
    lower_mask = jnp.tril(jnp.ones((GROUP, GROUP), bool))

    def advance(entering, scan_item):
        value_block, write_block, read_block, step_block = scan_item
        cumulative = jnp.cumsum(-rates[None, :] * step_block, axis=0)
        by_head = cumulative.T
        intersections = jnp.dot(read_block, write_block.T, preferred_element_type=jnp.float32)
        decay = jnp.exp(jnp.where(lower_mask[None], by_head[:, :, None] - by_head[:, None, :], -jnp.inf))
        mixing = (intersections[None] * decay * step_block.T[:, None, :]).astype(jnp.bfloat16)
        diagonal = jnp.einsum('hts,shp->thp', mixing.astype(jnp.float32), value_block.astype(jnp.float32), precision=lax.Precision.HIGHEST)
        carried = jnp.einsum('tn,hnp->thp', read_block.astype(jnp.float32), entering, precision=lax.Precision.HIGHEST) * jnp.exp(cumulative)[:, :, None]
        write_scale = jnp.exp(cumulative[-1][None, :] - cumulative) * step_block
        written = (write_block.astype(jnp.float32)[:, None, :] * write_scale[:, :, None]).astype(jnp.bfloat16)
        block_state = jnp.einsum('shn,shp->hnp', written.astype(jnp.float32), value_block.astype(jnp.float32), precision=lax.Precision.HIGHEST)
        result = diagonal + carried + skips[None, :, None] * value_block.astype(jnp.float32)
        leaving = jnp.exp(cumulative[-1])[:, None, None] * entering + block_state
        return (leaving, result.reshape(GROUP, HEADS * HEAD_SIZE))
    zero_state = jnp.zeros((HEADS, STATE, HEAD_SIZE), jnp.float32)
    ignored, results = lax.scan(advance, zero_state, (value_blocks, write_blocks, read_blocks, step_blocks))
    return results.reshape(total_rows, HEADS * HEAD_SIZE)

def rms_scale(matrix, gains):
    return matrix * lax.rsqrt(lax.optimization_barrier(jnp.mean(matrix * matrix, axis=-1, keepdims=True)) + 1e-05) * gains[None, :]

def reference(inner_first, gate_first, bc_first, first_raw_steps, rate_first, bias_first, skip_first, norm_gain, out_weight, residual, pre_gain, in_weight, conv_weight, conv_bias, step_weight, bias_second, rate_second, skip_second, final_gain):
    steps_one = jax.nn.softplus(first_raw_steps + bias_first[None, :])
    scanned_one = ssd(inner_first, bc_first[:, :STATE], bc_first[:, STATE:], steps_one, rate_first, skip_first)
    gated = scanned_one * jax.nn.silu(gate_first.astype(jnp.float32))
    normed_one = rms_scale(gated, norm_gain).astype(jnp.bfloat16)
    hidden_raster = (residual.astype(jnp.float32) + jnp.dot(normed_one, out_weight, preferred_element_type=jnp.float32)).astype(jnp.bfloat16)
    hidden_column = hidden_raster.reshape(GRID_ROWS, GRID_COLS, D).transpose(1, 0, 2).reshape(SAMPLE_TOKENS, D)
    pre_normed = rms_scale(hidden_column.astype(jnp.float32), pre_gain).astype(jnp.bfloat16)
    projected = jnp.dot(pre_normed, in_weight, preferred_element_type=jnp.float32).astype(jnp.bfloat16)
    padded = jnp.concatenate([jnp.zeros((KC - 1, projected.shape[1]), jnp.bfloat16), projected], axis=0)
    summed = conv_bias[None, :]
    for offset in range(KC):
        summed = summed + conv_weight[offset].astype(jnp.float32)[None, :] * padded[offset:offset + SAMPLE_TOKENS]
    convolved = jax.nn.silu(summed).astype(jnp.bfloat16)
    steps_two = jax.nn.softplus(jnp.dot(pre_normed, step_weight, preferred_element_type=jnp.float32) + bias_second[None, :])
    scanned_two = ssd(convolved[:, :INNER], convolved[:, INNER:INNER + STATE], convolved[:, INNER + STATE:], steps_two, rate_second, skip_second)
    return rms_scale(scanned_two, final_gain).astype(jnp.bfloat16)
```

```python
import functools

import jax
import jax.numpy as jnp
from jax import lax
from jax.experimental import pallas as pl
from jax.experimental.pallas import tpu as pltpu
from jax.sharding import PartitionSpec as P

KC = 4
COL_DEV = 1


def prefix(value, axis, combine, identity):
    peers, here = (lax.axis_size(axis), lax.axis_index(axis))
    everything = jax.tree.map(lambda part: lax.all_gather(part, axis), value)
    start = jax.tree.map(
        lambda part, zero: jnp.broadcast_to(jnp.asarray(zero, part.dtype), part.shape),
        value,
        identity,
    )

    def hop(k, before):
        reached = k < here
        new = combine(before, jax.tree.map(lambda part: part[k], everything))
        return jax.tree.map(lambda a, b: jnp.where(reached, a, b), new, before)

    return lax.fori_loop(0, peers, hop, start)


def shifted(value, axis, steps):
    count = lax.axis_size(axis)
    first, last = (max(0, -steps), min(count, count - steps))
    return lax.ppermute(value, axis, [(source, source + steps) for source in range(first, last)])


def chain_join(earlier, following):
    early_decay, early_state = earlier
    late_decay, late_state = following
    return (early_decay + late_decay, jnp.exp(late_decay)[:, None, None] * early_state + late_state)


def advance(entering, scan_item):
    block_decay, block_state = scan_item
    return (jnp.exp(block_decay)[:, None, None] * entering + block_state, entering)


def rms_scale(matrix, gains):
    return (
        matrix
        * lax.rsqrt(jnp.mean(matrix * matrix, axis=-1, keepdims=True) + 1e-05)
        * gains[None, :]
    )


def entering_state(device_decay, local_final):
    heads, state_width, head_width = local_final.shape
    zero_state = jnp.zeros((heads, state_width, head_width), jnp.float32)
    ignored, incoming = prefix(
        (device_decay, local_final),
        "tok",
        chain_join,
        (jnp.zeros((heads,), jnp.float32), zero_state),
    )
    return incoming


def ssd_local(values, write_side, read_side, steps, rates, skips):
    tok_rows = values.shape[0]
    heads = rates.shape[0]
    head_width = values.shape[1] // heads
    state_width = write_side.shape[1]
    block_len = min(256, tok_rows)
    blocks = tok_rows // block_len
    step_blocks = steps.reshape(blocks, block_len, heads)
    cumulative = jnp.cumsum(-rates[None, None, :] * step_blocks, axis=1)
    value_blocks = values.reshape(blocks, block_len, heads, head_width)
    write_blocks = write_side.reshape(blocks, block_len, state_width)
    read_blocks = read_side.reshape(blocks, block_len, state_width)
    write_scale = jnp.exp(cumulative[:, -1:, :] - cumulative) * step_blocks
    written = (write_blocks[:, :, None, :].astype(jnp.float32) * write_scale[:, :, :, None]).astype(
        jnp.bfloat16
    )
    block_states = jnp.einsum(
        "bqhn,bqhp->bhnp", written, value_blocks, preferred_element_type=jnp.float32
    )
    block_decay = cumulative[:, -1, :]
    zero_state = jnp.zeros((heads, state_width, head_width), jnp.float32)
    local_final, local_entry = lax.scan(advance, zero_state, (block_decay, block_states))
    device_decay = jnp.sum(block_decay, axis=0)
    incoming = entering_state(device_decay, local_final)
    decay_before = jnp.cumsum(block_decay, axis=0) - block_decay
    entry = local_entry + jnp.exp(decay_before)[:, :, None, None] * incoming[None]
    intersections = jnp.einsum(
        "btn,bsn->bts", read_blocks, write_blocks, preferred_element_type=jnp.float32
    )
    by_head = jnp.transpose(cumulative, (0, 2, 1))
    lower_mask = jnp.tril(jnp.ones((block_len, block_len), bool))
    decay = jnp.exp(
        jnp.where(lower_mask[None, None], by_head[:, :, :, None] - by_head[:, :, None, :], -jnp.inf)
    )
    step_heads = jnp.transpose(step_blocks, (0, 2, 1))
    mixing = (intersections[:, None] * decay * step_heads[:, :, None, :]).astype(jnp.bfloat16)
    diagonal = jnp.einsum(
        "bhts,bshp->bthp", mixing, value_blocks, preferred_element_type=jnp.float32
    )
    carried = (
        jnp.einsum(
            "btn,bhnp->bthp",
            read_blocks.astype(jnp.float32),
            entry,
            precision=lax.Precision.HIGHEST,
        )
        * jnp.exp(cumulative)[:, :, :, None]
    )
    result = diagonal + carried + skips[None, None, :, None] * value_blocks.astype(jnp.float32)
    return result.reshape(tok_rows, heads * head_width)


def local(
    inner_first,
    gate_first,
    bc_first,
    first_raw_steps,
    rate_first,
    bias_first,
    skip_first,
    norm_gain,
    out_weight,
    residual,
    pre_gain,
    in_weight,
    conv_weight,
    conv_bias,
    step_weight,
    bias_second,
    rate_second,
    skip_second,
    final_gain,
):
    state_width = bc_first.shape[1] // 2
    inner_width = inner_first.shape[1]
    model_width = residual.shape[1]
    out_whole, in_whole = (
        lax.all_gather(out_weight, "tok", axis=0, tiled=True),
        lax.all_gather(in_weight, "tok", axis=0, tiled=True),
    )
    steps_one = jax.nn.softplus(first_raw_steps + bias_first[None, :])
    scanned_one = ssd_local(
        inner_first,
        bc_first[:, :state_width],
        bc_first[:, state_width:],
        steps_one,
        rate_first,
        skip_first,
    )
    gated = scanned_one * jax.nn.silu(gate_first.astype(jnp.float32))
    normed_one = rms_scale(gated, norm_gain).astype(jnp.bfloat16)
    hidden_raster = (
        residual.astype(jnp.float32)
        + jnp.dot(normed_one, out_whole, preferred_element_type=jnp.float32)
    ).astype(jnp.bfloat16)
    tok_rows = hidden_raster.shape[0]
    peers = lax.axis_size("tok")
    raster_rows = tok_rows // (peers * COL_DEV)
    outgoing = hidden_raster.reshape(raster_rows, peers, COL_DEV, model_width).transpose(2, 1, 0, 3)
    arrived = lax.all_to_all(outgoing, "tok", split_axis=1, concat_axis=1, tiled=True)
    hidden_column = arrived.reshape(tok_rows, model_width)
    pre_normed = rms_scale(hidden_column.astype(jnp.float32), pre_gain).astype(jnp.bfloat16)
    rim_width = KC - 1
    projected = jnp.dot(pre_normed, in_whole, preferred_element_type=jnp.float32).astype(
        jnp.bfloat16
    )
    rim_projected = shifted(projected[tok_rows - rim_width :], "tok", 1)
    padded = jnp.concatenate([rim_projected, projected], axis=0)
    summed = conv_bias[None, :]
    for offset in range(KC):
        summed = (
            summed
            + conv_weight[offset].astype(jnp.float32)[None, :] * padded[offset : offset + tok_rows]
        )
    convolved = jax.nn.silu(summed).astype(jnp.bfloat16)
    steps_two = jax.nn.softplus(
        jnp.dot(pre_normed, step_weight, preferred_element_type=jnp.float32) + bias_second[None, :]
    )
    scanned_two = ssd_local(
        convolved[:, :inner_width],
        convolved[:, inner_width : inner_width + state_width],
        convolved[:, inner_width + state_width :],
        steps_two,
        rate_second,
        skip_second,
    )
    return rms_scale(scanned_two, final_gain).astype(jnp.bfloat16)


MESH = pl.DeviceIdType.MESH
BF = jnp.bfloat16
F32 = jnp.float32
INNER_K, BC_K, RAW_K, GATE_K, RES_K, SQ1_K, OUT_K, SQ2_K, VAL_K, PROJ_K, FIN_K = range(11)
KINDS = 11


def softplus(x):
    return jnp.maximum(x, 0.0) + jnp.log1p(jnp.exp(-jnp.abs(x)))


def as_column(row):
    rows = row.shape[1]
    return jnp.broadcast_to(row, (rows, rows)).T[:, 0:1]


def as_rows(column):
    rows = column.shape[0]
    return jnp.broadcast_to(column, (rows, rows)).T[0:8]


def ssd_heads(values, write_side, read_side, steps, rates, skips, heads, tmp):
    rows, width = values.shape
    head = width // heads
    at = lax.broadcasted_iota(jnp.int32, (rows, rows), 0)
    source = lax.broadcasted_iota(jnp.int32, (rows, rows), 1)
    ahead = (at <= source).astype(F32)
    cumulative = jnp.dot(
        -rates * steps, ahead, precision=lax.Precision.HIGHEST, preferred_element_type=F32
    )
    tmp[0:8, :] = cumulative
    columns = tmp[...].T
    scores = lax.dot_general(
        read_side, write_side, (((1,), (1,)), ((), ())), preferred_element_type=F32
    )
    lower = source <= at
    mixing = []
    for h in range(heads):
        gap = columns[:, h : h + 1] - cumulative[h : h + 1, :]
        decay = jnp.exp(jnp.where(lower, gap, -1e30))
        mixing.append((scores * decay * steps[h : h + 1, :]).astype(BF))
    product = jnp.dot(jnp.concatenate(mixing, axis=0), values, preferred_element_type=F32)
    owner = lax.broadcasted_iota(jnp.int32, (rows, width), 1) // head
    wide = values.astype(F32)
    result = jnp.zeros((rows, width), F32)
    for h in range(heads):
        part = product[h * rows : (h + 1) * rows] + skips[h : h + 1, :] * wide
        result = jnp.where(owner == h, part, result)
    return result


def fused(
    peers,
    heads,
    inner,
    gate,
    bc,
    raw,
    rate_one,
    bias_one,
    skip_one,
    norm_gain,
    out_hbm,
    residual,
    pre_gain,
    in_hbm,
    conv_weight,
    conv_bias,
    step_weight,
    bias_two,
    rate_two,
    skip_two,
    final_gain,
    result,
    out_w,
    in_w,
    inner_all,
    gate_all,
    bc_all,
    raw_all,
    res_all,
    out_tx,
    out_rx,
    sq1_tx,
    sq1_rx,
    val_tx,
    val_rx,
    proj_tx,
    proj_rx,
    sq2_tx,
    sq2_rx,
    fin_tx,
    fin,
    tmp,
    load_sem,
    send_sem,
    recv_sem,
):
    tok_rows, inner_width = inner.shape
    rows = tok_rows * peers
    slab = inner_width // peers
    state = bc.shape[1] // 2
    total_heads = heads * peers
    me = lax.axis_index("tok")
    order = [peers // 2]
    for d in range(1, peers // 2):
        order += [peers // 2 - d, peers // 2 + d]

    def peer(d):
        return lax.rem(me + d, peers)

    def at(index, size):
        return pl.ds(pl.multiple_of(index * size, size), size)

    flights = []

    def send(kind, d, src, dst):
        copy = pltpu.make_async_remote_copy(
            src_ref=src,
            dst_ref=dst,
            send_sem=send_sem.at[kind, d],
            recv_sem=recv_sem.at[kind, d],
            device_id={"tok": peer(d)},
            device_id_type=MESH,
        )
        copy.start()
        flights.append(copy)
        return copy

    load_out = pltpu.make_async_copy(out_hbm, out_w, load_sem.at[0])
    load_in = pltpu.make_async_copy(in_hbm, in_w, load_sem.at[1])
    load_out.start()
    load_in.start()
    barrier = pltpu.get_barrier_semaphore()
    for d in range(1, peers):
        pl.semaphore_signal(barrier, inc=1, device_id={"tok": peer(d)}, device_id_type=MESH)
    mine = at(me, slab)
    my_rows = at(me, tok_rows)
    inner_all[my_rows, :] = inner[:, mine]
    gate_all[my_rows, :] = gate[:, mine]
    res_all[my_rows, :] = residual[:, mine]
    bc_all[my_rows, :] = bc[...]
    raw_all[my_rows, :] = raw[...]
    tmp[...] = jnp.zeros_like(tmp)
    for index, ref in enumerate((rate_one, bias_one, skip_one, rate_two, bias_two, skip_two)):
        tmp[index : index + 1, 0:total_heads] = ref[...]
    lanes = tmp.shape[1]
    turn = lax.rem(lanes - me * heads, lanes)
    params = pltpu.roll(tmp[...], turn, 1).T
    pl.semaphore_wait(barrier, peers - 1)

    first = {}
    for d in order:
        first[RAW_K, d] = send(RAW_K, d, raw, raw_all.at[my_rows, :])
        first[BC_K, d] = send(BC_K, d, bc, bc_all.at[my_rows, :])
        first[INNER_K, d] = send(
            INNER_K, d, inner.at[:, at(peer(d), slab)], inner_all.at[my_rows, :]
        )
    for d in order:
        first[GATE_K, d] = send(GATE_K, d, gate.at[:, at(peer(d), slab)], gate_all.at[my_rows, :])
    for d in order:
        first[RES_K, d] = send(RES_K, d, residual.at[:, at(peer(d), slab)], res_all.at[my_rows, :])

    def arrived(copies, *kinds):
        for kind in kinds:
            for d in order:
                copies[kind, d].wait_recv()

    arrived(first, RAW_K)
    tmp[...] = jnp.zeros_like(tmp)
    tmp[:, 0:total_heads] = raw_all[...]
    steps = softplus(pltpu.roll(tmp[...], turn, 1).T[0:8] + params[0:8, 1:2])
    arrived(first, BC_K, INNER_K)
    scanned = ssd_heads(
        inner_all[...],
        bc_all[:, 0:state],
        bc_all[:, state : 2 * state],
        steps,
        params[0:8, 0:1],
        params[0:8, 2:3],
        heads,
        tmp,
    )
    arrived(first, GATE_K)
    gated = scanned * jax.nn.silu(gate_all[...].astype(F32))
    sq1_tx[...] = as_rows(jnp.sum(gated * gated, axis=1, keepdims=True))
    second = {}
    for d in order:
        second[SQ1_K, d] = send(SQ1_K, d, sq1_tx, sq1_rx.at[d])
    scaled = (gated * norm_gain[:, mine]).astype(BF)
    load_out.wait()
    for d in order:
        out_tx[d] = jnp.dot(
            scaled, out_w[:, at(peer(d), slab)], preferred_element_type=F32
        ).astype(BF)
        second[OUT_K, d] = send(OUT_K, d, out_tx.at[d], out_rx.at[d])
    hidden = jnp.dot(scaled, out_w[:, mine], preferred_element_type=F32)
    arrived(first, RES_K)
    arrived(second, SQ1_K)
    squares = sq1_tx[...]
    for d in order:
        squares = squares + sq1_rx[d]
    scale = as_column(lax.rsqrt(squares[0:1] / inner_width + 1e-05))
    for d in order:
        second[OUT_K, d].wait_recv()
        hidden = hidden + out_rx[d].astype(F32)
    hidden = (res_all[...].astype(F32) + scale * hidden).astype(BF)
    to = lax.broadcasted_iota(jnp.int32, (rows, rows), 0)
    raster = lax.broadcasted_iota(jnp.int32, (rows, rows), 1)
    moved = (raster % peers) * (rows // peers) + raster // peers
    hidden = jnp.dot((to == moved).astype(BF), hidden, preferred_element_type=F32)

    width = in_w.shape[1]
    pre = (hidden * pre_gain[:, mine]).astype(BF)
    tmp[...] = jnp.zeros_like(tmp)
    tmp[:, 0:total_heads] = jnp.dot(pre, step_weight[mine, :], preferred_element_type=F32)
    logits = tmp[...].T
    squares = as_rows(jnp.sum(hidden * hidden, axis=1, keepdims=True))
    for p in range(peers):
        sq2_tx[p, 0:heads, :] = logits[p * heads : (p + 1) * heads]
        sq2_tx[p, heads:8, :] = squares[heads:8]
    third = {}
    for d in order:
        third[SQ2_K, d] = send(SQ2_K, d, sq2_tx.at[peer(d)], sq2_rx.at[d])
    load_in.wait()
    proj = jnp.dot(pre, in_w[:, inner_width:width], preferred_element_type=F32)
    proj_tx[...] = proj.astype(BF)
    for d in order:
        third[PROJ_K, d] = send(PROJ_K, d, proj_tx, proj_rx.at[d])
    for d in order:
        val_tx[d] = jnp.dot(pre, in_w[:, at(peer(d), slab)], preferred_element_type=F32).astype(BF)
        third[VAL_K, d] = send(VAL_K, d, val_tx.at[d], val_rx.at[d])
    value = jnp.dot(pre, in_w[:, mine], preferred_element_type=F32)
    arrived(third, SQ2_K)
    gathered = sq2_tx[me]
    for d in order:
        gathered = gathered + sq2_rx[d]
    scale_row = lax.rsqrt(gathered[heads : heads + 1] / inner_width + 1e-05)
    scale = as_column(scale_row)
    steps = softplus(scale_row * gathered + params[0:8, 4:5])

    def convolve(projected, columns):
        projected = projected.astype(BF).astype(F32)
        taps = conv_weight[:, columns].astype(F32)
        place = lax.broadcasted_iota(jnp.int32, projected.shape, 0)
        total = conv_bias[:, columns]
        for offset in range(KC):
            back = KC - 1 - offset
            term = projected
            if back:
                term = jnp.where(place < back, 0.0, pltpu.roll(projected, back, 0))
            total = total + taps[offset : offset + 1] * term
        return jax.nn.silu(total).astype(BF)

    for d in order:
        third[PROJ_K, d].wait_recv()
        proj = proj + proj_rx[d].astype(F32)
    both = convolve(scale * proj, slice(inner_width, width))
    for d in order:
        third[VAL_K, d].wait_recv()
        value = value + val_rx[d].astype(F32)
    scanned = ssd_heads(
        convolve(scale * value, mine),
        both[:, 0:state],
        both[:, state : 2 * state],
        steps,
        params[0:8, 3:4],
        params[0:8, 5:6],
        heads,
        tmp,
    ).astype(BF)
    fin_tx[...] = scanned
    last = {}
    for d in order:
        last[FIN_K, d] = send(FIN_K, d, fin_tx.at[at(peer(d), tok_rows), :], fin.at[:, mine])
    fin[:, mine] = fin_tx[my_rows, :]
    arrived(last, FIN_K)
    result[...] = rms_scale(fin[...].astype(F32), final_gain[0]).astype(BF)
    for copy in flights:
        copy.wait_send()


def fused_local(peers, *args):
    (inner, gate, bc, raw, rate_one, bias_one, skip_one, norm_gain, out_w, residual) = args[:10]
    (pre_gain, in_w, conv_w, conv_bias, step_w, bias_two, rate_two, skip_two, final_gain) = args[10:]
    tok_rows, inner_width = inner.shape
    heads = rate_one.shape[0] // peers
    rows, slab = (tok_rows * peers, inner_width // peers)
    state2 = bc.shape[1]

    def flat(vector):
        return vector.reshape(1, vector.shape[0])

    vmem = pl.BlockSpec(memory_space=pltpu.VMEM)
    anywhere = pl.BlockSpec(memory_space=pl.ANY)
    specs = [vmem] * 19
    specs[8] = anywhere
    specs[11] = anywhere
    return pl.pallas_call(
        functools.partial(fused, peers, heads),
        out_shape=jax.ShapeDtypeStruct((tok_rows, inner_width), BF),
        in_specs=specs,
        out_specs=vmem,
        scratch_shapes=[
            pltpu.VMEM(out_w.shape, BF),
            pltpu.VMEM(in_w.shape, BF),
            pltpu.VMEM((rows, slab), BF),
            pltpu.VMEM((rows, slab), BF),
            pltpu.VMEM((rows, state2), BF),
            pltpu.VMEM((rows, raw.shape[1]), F32),
            pltpu.VMEM((rows, slab), BF),
            pltpu.VMEM((peers, rows, slab), BF),
            pltpu.VMEM((peers, rows, slab), BF),
            pltpu.VMEM((8, rows), F32),
            pltpu.VMEM((peers, 8, rows), F32),
            pltpu.VMEM((peers, rows, slab), BF),
            pltpu.VMEM((peers, rows, slab), BF),
            pltpu.VMEM((rows, state2), BF),
            pltpu.VMEM((peers, rows, state2), BF),
            pltpu.VMEM((peers, 8, rows), F32),
            pltpu.VMEM((peers, 8, rows), F32),
            pltpu.VMEM((rows, slab), BF),
            pltpu.VMEM((tok_rows, inner_width), BF),
            pltpu.VMEM((rows, rows), F32),
            pltpu.SemaphoreType.DMA((2,)),
            pltpu.SemaphoreType.DMA((KINDS, peers)),
            pltpu.SemaphoreType.DMA((KINDS, peers)),
        ],
        compiler_params=pltpu.CompilerParams(
            collective_id=0, has_side_effects=True, vmem_limit_bytes=40 * 1024 * 1024
        ),
    )(
        inner,
        gate,
        bc,
        raw,
        flat(rate_one),
        flat(bias_one),
        flat(skip_one),
        flat(norm_gain),
        out_w,
        residual,
        flat(pre_gain),
        in_w,
        conv_w,
        flat(conv_bias),
        step_w,
        flat(bias_two),
        flat(rate_two),
        flat(skip_two),
        flat(final_gain),
    )


def local_step(peers, *args):
    inner, bc, rates = (args[0], args[2], args[4])
    tok_rows, inner_width = inner.shape
    heads = rates.shape[0]
    fits = (
        tok_rows * peers == 128
        and tok_rows % 16 == 0
        and tok_rows % peers == 0
        and heads % peers == 0
        and heads // peers < 8
        and heads <= 128
        and inner_width % (128 * peers) == 0
        and args[9].shape[1] == inner_width
        and bc.shape[1] == 256
    )
    return fused_local(peers, *args) if fits else local(*args)


def solution(mesh):
    placed = (
        P(("batch", "tok"), None),
        P(("batch", "tok"), None),
        P(("batch", "tok"), None),
        P(("batch", "tok"), None),
        P(),
        P(),
        P(),
        P(),
        P("tok", None),
        P(("batch", "tok"), None),
        P(),
        P("tok", None),
        P(),
        P(),
        P(),
        P(),
        P(),
        P(),
        P(),
    )
    return jax.shard_map(
        functools.partial(local_step, mesh.shape["tok"]), mesh=mesh, in_specs=placed, out_specs=P(("batch", "tok"), None), check_vma=False
    )
```

```python
import functools

import jax
import jax.numpy as jnp
from jax import lax
from jax.experimental import pallas as pl
from jax.experimental.pallas import tpu as pltpu
from jax.sharding import PartitionSpec as P

KC = 4
COL_DEV = 1


def prefix(value, axis, combine, identity):
    peers, here = (lax.axis_size(axis), lax.axis_index(axis))
    everything = jax.tree.map(lambda part: lax.all_gather(part, axis), value)
    start = jax.tree.map(
        lambda part, zero: jnp.broadcast_to(jnp.asarray(zero, part.dtype), part.shape),
        value,
        identity,
    )

    def hop(k, before):
        reached = k < here
        new = combine(before, jax.tree.map(lambda part: part[k], everything))
        return jax.tree.map(lambda a, b: jnp.where(reached, a, b), new, before)

    return lax.fori_loop(0, peers, hop, start)


def shifted(value, axis, steps):
    count = lax.axis_size(axis)
    first, last = (max(0, -steps), min(count, count - steps))
    return lax.ppermute(value, axis, [(source, source + steps) for source in range(first, last)])


def chain_join(earlier, following):
    early_decay, early_state = earlier
    late_decay, late_state = following
    return (early_decay + late_decay, jnp.exp(late_decay)[:, None, None] * early_state + late_state)


def advance(entering, scan_item):
    block_decay, block_state = scan_item
    return (jnp.exp(block_decay)[:, None, None] * entering + block_state, entering)


def rms_scale(matrix, gains):
    return (
        matrix
        * lax.rsqrt(jnp.mean(matrix * matrix, axis=-1, keepdims=True) + 1e-05)
        * gains[None, :]
    )


def entering_state(device_decay, local_final):
    heads, state_width, head_width = local_final.shape
    zero_state = jnp.zeros((heads, state_width, head_width), jnp.float32)
    ignored, incoming = prefix(
        (device_decay, local_final),
        "tok",
        chain_join,
        (jnp.zeros((heads,), jnp.float32), zero_state),
    )
    return incoming


def ssd_local(values, write_side, read_side, steps, rates, skips):
    tok_rows = values.shape[0]
    heads = rates.shape[0]
    head_width = values.shape[1] // heads
    state_width = write_side.shape[1]
    block_len = min(256, tok_rows)
    blocks = tok_rows // block_len
    step_blocks = steps.reshape(blocks, block_len, heads)
    cumulative = jnp.cumsum(-rates[None, None, :] * step_blocks, axis=1)
    value_blocks = values.reshape(blocks, block_len, heads, head_width)
    write_blocks = write_side.reshape(blocks, block_len, state_width)
    read_blocks = read_side.reshape(blocks, block_len, state_width)
    write_scale = jnp.exp(cumulative[:, -1:, :] - cumulative) * step_blocks
    written = (write_blocks[:, :, None, :].astype(jnp.float32) * write_scale[:, :, :, None]).astype(
        jnp.bfloat16
    )
    block_states = jnp.einsum(
        "bqhn,bqhp->bhnp", written, value_blocks, preferred_element_type=jnp.float32
    )
    block_decay = cumulative[:, -1, :]
    zero_state = jnp.zeros((heads, state_width, head_width), jnp.float32)
    local_final, local_entry = lax.scan(advance, zero_state, (block_decay, block_states))
    device_decay = jnp.sum(block_decay, axis=0)
    incoming = entering_state(device_decay, local_final)
    decay_before = jnp.cumsum(block_decay, axis=0) - block_decay
    entry = local_entry + jnp.exp(decay_before)[:, :, None, None] * incoming[None]
    intersections = jnp.einsum(
        "btn,bsn->bts", read_blocks, write_blocks, preferred_element_type=jnp.float32
    )
    by_head = jnp.transpose(cumulative, (0, 2, 1))
    lower_mask = jnp.tril(jnp.ones((block_len, block_len), bool))
    decay = jnp.exp(
        jnp.where(lower_mask[None, None], by_head[:, :, :, None] - by_head[:, :, None, :], -jnp.inf)
    )
    step_heads = jnp.transpose(step_blocks, (0, 2, 1))
    mixing = (intersections[:, None] * decay * step_heads[:, :, None, :]).astype(jnp.bfloat16)
    diagonal = jnp.einsum(
        "bhts,bshp->bthp", mixing, value_blocks, preferred_element_type=jnp.float32
    )
    carried = (
        jnp.einsum(
            "btn,bhnp->bthp",
            read_blocks.astype(jnp.float32),
            entry,
            precision=lax.Precision.HIGHEST,
        )
        * jnp.exp(cumulative)[:, :, :, None]
    )
    result = diagonal + carried + skips[None, None, :, None] * value_blocks.astype(jnp.float32)
    return result.reshape(tok_rows, heads * head_width)


def local(
    inner_first,
    gate_first,
    bc_first,
    first_raw_steps,
    rate_first,
    bias_first,
    skip_first,
    norm_gain,
    out_weight,
    residual,
    pre_gain,
    in_weight,
    conv_weight,
    conv_bias,
    step_weight,
    bias_second,
    rate_second,
    skip_second,
    final_gain,
):
    state_width = bc_first.shape[1] // 2
    inner_width = inner_first.shape[1]
    model_width = residual.shape[1]
    out_whole, in_whole = (
        lax.all_gather(out_weight, "tok", axis=0, tiled=True),
        lax.all_gather(in_weight, "tok", axis=0, tiled=True),
    )
    steps_one = jax.nn.softplus(first_raw_steps + bias_first[None, :])
    scanned_one = ssd_local(
        inner_first,
        bc_first[:, :state_width],
        bc_first[:, state_width:],
        steps_one,
        rate_first,
        skip_first,
    )
    gated = scanned_one * jax.nn.silu(gate_first.astype(jnp.float32))
    normed_one = rms_scale(gated, norm_gain).astype(jnp.bfloat16)
    hidden_raster = (
        residual.astype(jnp.float32)
        + jnp.dot(normed_one, out_whole, preferred_element_type=jnp.float32)
    ).astype(jnp.bfloat16)
    tok_rows = hidden_raster.shape[0]
    peers = lax.axis_size("tok")
    raster_rows = tok_rows // (peers * COL_DEV)
    outgoing = hidden_raster.reshape(raster_rows, peers, COL_DEV, model_width).transpose(2, 1, 0, 3)
    arrived = lax.all_to_all(outgoing, "tok", split_axis=1, concat_axis=1, tiled=True)
    hidden_column = arrived.reshape(tok_rows, model_width)
    pre_normed = rms_scale(hidden_column.astype(jnp.float32), pre_gain).astype(jnp.bfloat16)
    rim_width = KC - 1
    projected = jnp.dot(pre_normed, in_whole, preferred_element_type=jnp.float32).astype(
        jnp.bfloat16
    )
    rim_projected = shifted(projected[tok_rows - rim_width :], "tok", 1)
    padded = jnp.concatenate([rim_projected, projected], axis=0)
    summed = conv_bias[None, :]
    for offset in range(KC):
        summed = (
            summed
            + conv_weight[offset].astype(jnp.float32)[None, :] * padded[offset : offset + tok_rows]
        )
    convolved = jax.nn.silu(summed).astype(jnp.bfloat16)
    steps_two = jax.nn.softplus(
        jnp.dot(pre_normed, step_weight, preferred_element_type=jnp.float32) + bias_second[None, :]
    )
    scanned_two = ssd_local(
        convolved[:, :inner_width],
        convolved[:, inner_width : inner_width + state_width],
        convolved[:, inner_width + state_width :],
        steps_two,
        rate_second,
        skip_second,
    )
    return rms_scale(scanned_two, final_gain).astype(jnp.bfloat16)


MESH = pl.DeviceIdType.MESH
BF = jnp.bfloat16
F32 = jnp.float32
INNER_K, BC_K, RAW_K, GATE_K, RES_K, SQ1_K, OUT_K, SQ2_K, VAL_K, PROJ_K, SPREAD_K, FIN_K = range(12)
KINDS = 12
LOADS = 19


def softplus(x):
    return jnp.maximum(x, 0.0) + jnp.log1p(jnp.exp(-jnp.abs(x)))


def as_column(row):
    rows = row.shape[1]
    return jnp.broadcast_to(row, (rows, rows)).T[:, 0:1]


def as_rows(column):
    rows = column.shape[0]
    return jnp.broadcast_to(column, (rows, rows)).T[0:8]


def ssd_heads(values, write_side, read_side, steps, rates, skips, heads, tmp):
    rows, width = values.shape
    head = width // heads
    at = lax.broadcasted_iota(jnp.int32, (rows, rows), 0)
    source = lax.broadcasted_iota(jnp.int32, (rows, rows), 1)
    ahead = (at <= source).astype(F32)
    cumulative = jnp.dot(
        -rates * steps, ahead, precision=lax.Precision.HIGHEST, preferred_element_type=F32
    )
    tmp[0:8, :] = cumulative
    columns = tmp[...].T
    scores = lax.dot_general(
        read_side, write_side, (((1,), (1,)), ((), ())), preferred_element_type=F32
    )
    lower = source <= at
    mixing = []
    for h in range(heads):
        gap = columns[:, h : h + 1] - cumulative[h : h + 1, :]
        decay = jnp.exp(jnp.where(lower, gap, -1e30))
        mixing.append((scores * decay * steps[h : h + 1, :]).astype(BF))
    product = jnp.dot(jnp.concatenate(mixing, axis=0), values, preferred_element_type=F32)
    owner = lax.broadcasted_iota(jnp.int32, (rows, width), 1) // head
    wide = values.astype(F32)
    result = jnp.zeros((rows, width), F32)
    for h in range(heads):
        part = product[h * rows : (h + 1) * rows] + skips[h : h + 1, :] * wide
        result = jnp.where(owner == h, part, result)
    return result


def fused(peers, heads, *refs):
    (inner, gate, bc, raw), (residual,), small_hbm = (refs[0:4], refs[4:5], refs[5:19])
    result, small = (refs[19], refs[20:34])
    (rate_one, bias_one, skip_one, rate_two, bias_two, skip_two) = small[0:6]
    (out_w, norm_gain, pre_gain, in_w, step_weight, conv_weight, conv_bias, final_gain) = small[6:14]
    (inner_all, gate_all, bc_all, raw_all, res_all, out_tx, out_rx, sq1_tx, sq1_rx) = refs[34:43]
    (val_tx, val_rx, proj_tx, proj_rx, spread_tx, proj_all, sq2_tx, sq2_rx) = refs[43:51]
    (fin_tx, fin, tmp, load_sem, send_sem, recv_sem) = refs[51:57]
    tok_rows, inner_width = inner.shape
    rows = tok_rows * peers
    slab = inner_width // peers
    state = bc.shape[1] // 2
    total_heads = heads * peers
    me = lax.axis_index("tok")
    order = [peers // 2]
    for d in range(1, peers // 2):
        order += [peers // 2 - d, peers // 2 + d]

    def peer(d):
        return lax.rem(me + d, peers)

    def at(index, size):
        return pl.ds(pl.multiple_of(index * size, size), size)

    flights = []

    def send(kind, d, src, dst):
        copy = pltpu.make_async_remote_copy(
            src_ref=src,
            dst_ref=dst,
            send_sem=send_sem.at[kind, d],
            recv_sem=recv_sem.at[kind, d],
            device_id={"tok": peer(d)},
            device_id_type=MESH,
        )
        copy.start()
        flights.append(copy)
        return copy

    mine = at(me, slab)
    my_rows = at(me, tok_rows)
    loads = [
        pltpu.make_async_copy(source, target, load_sem.at[index])
        for index, (source, target) in enumerate(
            [
                (raw, raw_all.at[my_rows, :]),
                (bc, bc_all.at[my_rows, :]),
                (inner.at[:, mine], inner_all.at[my_rows, :]),
                (gate.at[:, mine], gate_all.at[my_rows, :]),
                (residual.at[:, mine], res_all.at[my_rows, :]),
                *zip(small_hbm, small),
            ]
        )
    ]
    for load in loads:
        load.start()
    barrier = pltpu.get_barrier_semaphore()
    for d in range(1, peers):
        pl.semaphore_signal(barrier, inc=1, device_id={"tok": peer(d)}, device_id_type=MESH)
    pl.semaphore_wait(barrier, peers - 1)

    first = {}
    for d in order:
        first[RAW_K, d] = send(RAW_K, d, raw, raw_all.at[my_rows, :])
        first[BC_K, d] = send(BC_K, d, bc, bc_all.at[my_rows, :])
        first[INNER_K, d] = send(
            INNER_K, d, inner.at[:, at(peer(d), slab)], inner_all.at[my_rows, :]
        )
    for d in order:
        first[GATE_K, d] = send(GATE_K, d, gate.at[:, at(peer(d), slab)], gate_all.at[my_rows, :])
    for d in order:
        first[RES_K, d] = send(RES_K, d, residual.at[:, at(peer(d), slab)], res_all.at[my_rows, :])

    def arrived(copies, *kinds):
        for kind in kinds:
            for d in order:
                copies[kind, d].wait_recv()

    tmp[...] = jnp.zeros_like(tmp)
    for load in loads[5:11]:
        load.wait()
    for index, ref in enumerate((rate_one, bias_one, skip_one, rate_two, bias_two, skip_two)):
        tmp[index : index + 1, 0:total_heads] = ref[...]
    lanes = tmp.shape[1]
    turn = lax.rem(lanes - me * heads, lanes)
    params = pltpu.roll(tmp[...], turn, 1).T
    tmp[...] = jnp.zeros_like(tmp)
    loads[0].wait()
    arrived(first, RAW_K)
    tmp[:, 0:total_heads] = raw_all[...]
    steps = softplus(pltpu.roll(tmp[...], turn, 1).T[0:8] + params[0:8, 1:2])
    loads[1].wait()
    loads[2].wait()
    arrived(first, BC_K, INNER_K)
    scanned = ssd_heads(
        inner_all[...],
        bc_all[:, 0:state],
        bc_all[:, state : 2 * state],
        steps,
        params[0:8, 0:1],
        params[0:8, 2:3],
        heads,
        tmp,
    )
    loads[3].wait()
    arrived(first, GATE_K)
    gated = scanned * jax.nn.silu(gate_all[...].astype(F32))
    sq1_tx[...] = as_rows(jnp.sum(gated * gated, axis=1, keepdims=True))
    second = {}
    for d in order:
        second[SQ1_K, d] = send(SQ1_K, d, sq1_tx, sq1_rx.at[d])
    loads[11].wait()
    loads[12].wait()
    scaled = (gated * norm_gain[:, mine]).astype(BF)
    for d in order:
        out_tx[d] = jnp.dot(
            scaled, out_w[:, at(peer(d), slab)], preferred_element_type=F32
        ).astype(BF)
        second[OUT_K, d] = send(OUT_K, d, out_tx.at[d], out_rx.at[d])
    hidden = jnp.dot(scaled, out_w[:, mine], preferred_element_type=F32)
    loads[4].wait()
    arrived(first, RES_K)
    arrived(second, SQ1_K)
    squares = sq1_tx[...]
    for d in order:
        squares = squares + sq1_rx[d]
    scale = as_column(lax.rsqrt(squares[0:1] / inner_width + 1e-05))
    for d in order:
        second[OUT_K, d].wait_recv()
        hidden = hidden + out_rx[d].astype(F32)
    hidden = (res_all[...].astype(F32) + scale * hidden).astype(BF)
    to = lax.broadcasted_iota(jnp.int32, (rows, rows), 0)
    raster = lax.broadcasted_iota(jnp.int32, (rows, rows), 1)
    moved = (raster % peers) * (rows // peers) + raster // peers
    hidden = jnp.dot((to == moved).astype(BF), hidden, preferred_element_type=F32)

    width = in_w.shape[1]
    for load in loads[13:19]:
        load.wait()
    pre = (hidden * pre_gain[:, mine]).astype(BF)
    logits = lax.dot_general(
        step_weight[:, mine], pre, (((1,), (1,)), ((), ())), preferred_element_type=F32
    )
    squares = as_rows(jnp.sum(hidden * hidden, axis=1, keepdims=True))
    for p in range(peers):
        sq2_tx[p, 0:heads, :] = logits[p * heads : (p + 1) * heads]
        sq2_tx[p, heads:8, :] = squares[heads:8]
    third = {}
    for d in order:
        third[SQ2_K, d] = send(SQ2_K, d, sq2_tx.at[peer(d)], sq2_rx.at[d])
    proj_tx[...] = jnp.dot(
        pre, in_w[:, inner_width:width], preferred_element_type=F32
    ).astype(BF)
    for d in order:
        third[PROJ_K, d] = send(
            PROJ_K, d, proj_tx.at[at(peer(d), tok_rows), :], proj_rx.at[d]
        )

    def send_values(d):
        val_tx[d] = jnp.dot(pre, in_w[:, at(peer(d), slab)], preferred_element_type=F32).astype(BF)
        third[VAL_K, d] = send(VAL_K, d, val_tx.at[d], val_rx.at[d])

    for d in order[0:4]:
        send_values(d)
    proj = proj_tx[my_rows, :].astype(F32)
    for d in order:
        third[PROJ_K, d].wait_recv()
        proj = proj + proj_rx[d].astype(F32)
    spread_tx[...] = proj.astype(BF)
    for d in order:
        third[SPREAD_K, d] = send(SPREAD_K, d, spread_tx, proj_all.at[my_rows, :])
    proj_all[my_rows, :] = spread_tx[...]
    for d in order[4:]:
        send_values(d)
    value = jnp.dot(pre, in_w[:, mine], preferred_element_type=F32)
    arrived(third, SQ2_K)
    gathered = sq2_tx[me]
    for d in order:
        gathered = gathered + sq2_rx[d]
    scale_row = lax.rsqrt(gathered[heads : heads + 1] / inner_width + 1e-05)
    scale = as_column(scale_row)
    steps = softplus(scale_row * gathered + params[0:8, 4:5])

    def convolve(projected, columns):
        taps = conv_weight[:, columns].astype(F32)
        place = lax.broadcasted_iota(jnp.int32, projected.shape, 0)
        total = conv_bias[:, columns]
        for offset in range(KC):
            back = KC - 1 - offset
            term = projected
            if back:
                term = jnp.where(place < back, 0.0, pltpu.roll(projected, back, 0))
            total = total + taps[offset : offset + 1] * term
        return jax.nn.silu(total).astype(BF)

    arrived(third, SPREAD_K)
    both = convolve(scale * proj_all[...].astype(F32), slice(inner_width, width))
    for d in order:
        third[VAL_K, d].wait_recv()
        value = value + val_rx[d].astype(F32)
    scanned = ssd_heads(
        convolve(scale * value, mine),
        both[:, 0:state],
        both[:, state : 2 * state],
        steps,
        params[0:8, 3:4],
        params[0:8, 5:6],
        heads,
        tmp,
    ).astype(BF)
    fin_tx[...] = scanned
    last = {}
    for d in order:
        last[FIN_K, d] = send(FIN_K, d, fin_tx.at[at(peer(d), tok_rows), :], fin.at[:, mine])
    fin[:, mine] = fin_tx[my_rows, :]
    arrived(last, FIN_K)
    result[...] = rms_scale(fin[...].astype(F32), final_gain[0]).astype(BF)
    for copy in flights:
        copy.wait_send()


def fused_local(peers, *args):
    (inner, gate, bc, raw, rate_one, bias_one, skip_one, norm_gain, out_w, residual) = args[:10]
    (pre_gain, in_w, conv_w, conv_bias, step_w, bias_two, rate_two, skip_two, final_gain) = args[10:]
    tok_rows, inner_width = inner.shape
    heads = rate_one.shape[0] // peers
    rows, slab = (tok_rows * peers, inner_width // peers)
    state2 = bc.shape[1]

    def flat(vector):
        return vector.reshape(1, vector.shape[0])

    big = (inner, gate, bc, raw, residual)
    small = tuple(map(flat, (rate_one, bias_one, skip_one, rate_two, bias_two, skip_two)))
    small += (out_w, flat(norm_gain), flat(pre_gain), in_w, step_w.T, conv_w)
    small += (flat(conv_bias), flat(final_gain))
    block = pltpu.VMEM((rows, slab), BF)
    blocks = pltpu.VMEM((peers, rows, slab), BF)
    tiles = pltpu.VMEM((peers, 8, rows), F32)
    sends = pltpu.SemaphoreType.DMA((KINDS, peers))
    return pl.pallas_call(
        functools.partial(fused, peers, heads),
        out_shape=jax.ShapeDtypeStruct((tok_rows, inner_width), BF),
        in_specs=[pl.BlockSpec(memory_space=pltpu.HBM)] * (len(big) + len(small)),
        out_specs=pl.BlockSpec(memory_space=pltpu.VMEM),
        scratch_shapes=[pltpu.VMEM(part.shape, part.dtype) for part in small]
        + [
            block,
            block,
            pltpu.VMEM((rows, state2), BF),
            pltpu.VMEM((rows, raw.shape[1]), F32),
            block,
            blocks,
            blocks,
            pltpu.VMEM((8, rows), F32),
            tiles,
            blocks,
            blocks,
            pltpu.VMEM((rows, state2), BF),
            pltpu.VMEM((peers, tok_rows, state2), BF),
            pltpu.VMEM((tok_rows, state2), BF),
            pltpu.VMEM((rows, state2), BF),
            tiles,
            tiles,
            block,
            pltpu.VMEM((tok_rows, inner_width), BF),
            pltpu.VMEM((rows, rows), F32),
            pltpu.SemaphoreType.DMA((LOADS,)),
            sends,
            sends,
        ],
        compiler_params=pltpu.CompilerParams(
            collective_id=0, has_side_effects=True, vmem_limit_bytes=60 * 1024 * 1024
        ),
    )(*big, *small)


def local_step(peers, *args):
    inner, bc, rates = (args[0], args[2], args[4])
    tok_rows, inner_width = inner.shape
    heads = rates.shape[0]
    fits = (
        tok_rows * peers == 128
        and tok_rows % 16 == 0
        and tok_rows % peers == 0
        and heads % peers == 0
        and heads // peers < 8
        and heads <= 128
        and inner_width % (128 * peers) == 0
        and args[9].shape[1] == inner_width
        and bc.shape[1] == 256
    )
    return fused_local(peers, *args) if fits else local(*args)


def solution(mesh):
    placed = (
        P(("batch", "tok"), None),
        P(("batch", "tok"), None),
        P(("batch", "tok"), None),
        P(("batch", "tok"), None),
        P(),
        P(),
        P(),
        P(),
        P("tok", None),
        P(("batch", "tok"), None),
        P(),
        P("tok", None),
        P(),
        P(),
        P(),
        P(),
        P(),
        P(),
        P(),
    )
    return jax.shard_map(
        functools.partial(local_step, mesh.shape["tok"]), mesh=mesh, in_specs=placed, out_specs=P(("batch", "tok"), None), check_vma=False
    )
```

```python
import functools

import jax
import jax.numpy as jnp
from jax import lax
from jax.experimental import pallas as pl
from jax.experimental.pallas import tpu as pltpu
from jax.sharding import PartitionSpec as P

KC = 4
COL_DEV = 1


def prefix(value, axis, combine, identity):
    peers, here = (lax.axis_size(axis), lax.axis_index(axis))
    everything = jax.tree.map(lambda part: lax.all_gather(part, axis), value)
    start = jax.tree.map(
        lambda part, zero: jnp.broadcast_to(jnp.asarray(zero, part.dtype), part.shape),
        value,
        identity,
    )

    def hop(k, before):
        reached = k < here
        new = combine(before, jax.tree.map(lambda part: part[k], everything))
        return jax.tree.map(lambda a, b: jnp.where(reached, a, b), new, before)

    return lax.fori_loop(0, peers, hop, start)


def shifted(value, axis, steps):
    count = lax.axis_size(axis)
    first, last = (max(0, -steps), min(count, count - steps))
    return lax.ppermute(value, axis, [(source, source + steps) for source in range(first, last)])


def chain_join(earlier, following):
    early_decay, early_state = earlier
    late_decay, late_state = following
    return (early_decay + late_decay, jnp.exp(late_decay)[:, None, None] * early_state + late_state)


def advance(entering, scan_item):
    block_decay, block_state = scan_item
    return (jnp.exp(block_decay)[:, None, None] * entering + block_state, entering)


def rms_scale(matrix, gains):
    return (
        matrix
        * lax.rsqrt(jnp.mean(matrix * matrix, axis=-1, keepdims=True) + 1e-05)
        * gains[None, :]
    )


def entering_state(device_decay, local_final):
    heads, state_width, head_width = local_final.shape
    zero_state = jnp.zeros((heads, state_width, head_width), jnp.float32)
    ignored, incoming = prefix(
        (device_decay, local_final),
        "tok",
        chain_join,
        (jnp.zeros((heads,), jnp.float32), zero_state),
    )
    return incoming


def ssd_local(values, write_side, read_side, steps, rates, skips):
    tok_rows = values.shape[0]
    heads = rates.shape[0]
    head_width = values.shape[1] // heads
    state_width = write_side.shape[1]
    block_len = min(256, tok_rows)
    blocks = tok_rows // block_len
    step_blocks = steps.reshape(blocks, block_len, heads)
    cumulative = jnp.cumsum(-rates[None, None, :] * step_blocks, axis=1)
    value_blocks = values.reshape(blocks, block_len, heads, head_width)
    write_blocks = write_side.reshape(blocks, block_len, state_width)
    read_blocks = read_side.reshape(blocks, block_len, state_width)
    write_scale = jnp.exp(cumulative[:, -1:, :] - cumulative) * step_blocks
    written = (write_blocks[:, :, None, :].astype(jnp.float32) * write_scale[:, :, :, None]).astype(
        jnp.bfloat16
    )
    block_states = jnp.einsum(
        "bqhn,bqhp->bhnp", written, value_blocks, preferred_element_type=jnp.float32
    )
    block_decay = cumulative[:, -1, :]
    zero_state = jnp.zeros((heads, state_width, head_width), jnp.float32)
    local_final, local_entry = lax.scan(advance, zero_state, (block_decay, block_states))
    device_decay = jnp.sum(block_decay, axis=0)
    incoming = entering_state(device_decay, local_final)
    decay_before = jnp.cumsum(block_decay, axis=0) - block_decay
    entry = local_entry + jnp.exp(decay_before)[:, :, None, None] * incoming[None]
    intersections = jnp.einsum(
        "btn,bsn->bts", read_blocks, write_blocks, preferred_element_type=jnp.float32
    )
    by_head = jnp.transpose(cumulative, (0, 2, 1))
    lower_mask = jnp.tril(jnp.ones((block_len, block_len), bool))
    decay = jnp.exp(
        jnp.where(lower_mask[None, None], by_head[:, :, :, None] - by_head[:, :, None, :], -jnp.inf)
    )
    step_heads = jnp.transpose(step_blocks, (0, 2, 1))
    mixing = (intersections[:, None] * decay * step_heads[:, :, None, :]).astype(jnp.bfloat16)
    diagonal = jnp.einsum(
        "bhts,bshp->bthp", mixing, value_blocks, preferred_element_type=jnp.float32
    )
    carried = (
        jnp.einsum(
            "btn,bhnp->bthp",
            read_blocks.astype(jnp.float32),
            entry,
            precision=lax.Precision.HIGHEST,
        )
        * jnp.exp(cumulative)[:, :, :, None]
    )
    result = diagonal + carried + skips[None, None, :, None] * value_blocks.astype(jnp.float32)
    return result.reshape(tok_rows, heads * head_width)


def local(
    inner_first,
    gate_first,
    bc_first,
    first_raw_steps,
    rate_first,
    bias_first,
    skip_first,
    norm_gain,
    out_weight,
    residual,
    pre_gain,
    in_weight,
    conv_weight,
    conv_bias,
    step_weight,
    bias_second,
    rate_second,
    skip_second,
    final_gain,
):
    state_width = bc_first.shape[1] // 2
    inner_width = inner_first.shape[1]
    model_width = residual.shape[1]
    out_whole, in_whole = (
        lax.all_gather(out_weight, "tok", axis=0, tiled=True),
        lax.all_gather(in_weight, "tok", axis=0, tiled=True),
    )
    steps_one = jax.nn.softplus(first_raw_steps + bias_first[None, :])
    scanned_one = ssd_local(
        inner_first,
        bc_first[:, :state_width],
        bc_first[:, state_width:],
        steps_one,
        rate_first,
        skip_first,
    )
    gated = scanned_one * jax.nn.silu(gate_first.astype(jnp.float32))
    normed_one = rms_scale(gated, norm_gain).astype(jnp.bfloat16)
    hidden_raster = (
        residual.astype(jnp.float32)
        + jnp.dot(normed_one, out_whole, preferred_element_type=jnp.float32)
    ).astype(jnp.bfloat16)
    tok_rows = hidden_raster.shape[0]
    peers = lax.axis_size("tok")
    raster_rows = tok_rows // (peers * COL_DEV)
    outgoing = hidden_raster.reshape(raster_rows, peers, COL_DEV, model_width).transpose(2, 1, 0, 3)
    arrived = lax.all_to_all(outgoing, "tok", split_axis=1, concat_axis=1, tiled=True)
    hidden_column = arrived.reshape(tok_rows, model_width)
    pre_normed = rms_scale(hidden_column.astype(jnp.float32), pre_gain).astype(jnp.bfloat16)
    rim_width = KC - 1
    projected = jnp.dot(pre_normed, in_whole, preferred_element_type=jnp.float32).astype(
        jnp.bfloat16
    )
    rim_projected = shifted(projected[tok_rows - rim_width :], "tok", 1)
    padded = jnp.concatenate([rim_projected, projected], axis=0)
    summed = conv_bias[None, :]
    for offset in range(KC):
        summed = (
            summed
            + conv_weight[offset].astype(jnp.float32)[None, :] * padded[offset : offset + tok_rows]
        )
    convolved = jax.nn.silu(summed).astype(jnp.bfloat16)
    steps_two = jax.nn.softplus(
        jnp.dot(pre_normed, step_weight, preferred_element_type=jnp.float32) + bias_second[None, :]
    )
    scanned_two = ssd_local(
        convolved[:, :inner_width],
        convolved[:, inner_width : inner_width + state_width],
        convolved[:, inner_width + state_width :],
        steps_two,
        rate_second,
        skip_second,
    )
    return rms_scale(scanned_two, final_gain).astype(jnp.bfloat16)


MESH = pl.DeviceIdType.MESH
BF = jnp.bfloat16
F32 = jnp.float32
INNER_K, BC_K, RAW_K, GATE_K, RES_K, SQ1_K, OUT_K, SQ2_K, VAL_K, PROJ_K, SPREAD_K, FIN_K = range(12)
KINDS = 12
LOADS = 19


def softplus(x):
    return jnp.maximum(x, 0.0) + jnp.log1p(jnp.exp(-jnp.abs(x)))


def as_column(row):
    rows = row.shape[1]
    return jnp.broadcast_to(row, (rows, rows)).T[:, 0:1]


def as_rows(column):
    rows = column.shape[0]
    return jnp.broadcast_to(column, (rows, rows)).T[0:8]


def ssd_heads(values, write_side, read_side, steps, rates, skips, heads, tmp):
    rows, width = values.shape
    head = width // heads
    at = lax.broadcasted_iota(jnp.int32, (rows, rows), 0)
    source = lax.broadcasted_iota(jnp.int32, (rows, rows), 1)
    ahead = (at <= source).astype(F32)
    cumulative = jnp.dot(
        -rates * steps, ahead, precision=lax.Precision.HIGHEST, preferred_element_type=F32
    )
    tmp[0:8, :] = cumulative
    columns = tmp[...].T
    scores = lax.dot_general(
        read_side, write_side, (((1,), (1,)), ((), ())), preferred_element_type=F32
    )
    lower = source <= at
    mixing = []
    for h in range(heads):
        gap = columns[:, h : h + 1] - cumulative[h : h + 1, :]
        decay = jnp.exp(jnp.where(lower, gap, -1e30))
        mixing.append((scores * decay * steps[h : h + 1, :]).astype(BF))
    product = jnp.dot(jnp.concatenate(mixing, axis=0), values, preferred_element_type=F32)
    owner = lax.broadcasted_iota(jnp.int32, (rows, width), 1) // head
    wide = values.astype(F32)
    result = jnp.zeros((rows, width), F32)
    for h in range(heads):
        part = product[h * rows : (h + 1) * rows] + skips[h : h + 1, :] * wide
        result = jnp.where(owner == h, part, result)
    return result


def fused(peers, heads, *refs):
    (inner, gate, bc, raw), (residual,), small_hbm = (refs[0:4], refs[4:5], refs[5:19])
    result, small = (refs[19], refs[20:34])
    (rate_one, bias_one, skip_one, rate_two, bias_two, skip_two) = small[0:6]
    (out_w, norm_gain, pre_gain, in_w, step_weight, conv_weight, conv_bias, final_gain) = small[6:14]
    (inner_all, gate_all, bc_all, raw_all, res_all, out_tx, out_rx, sq1_tx, sq1_rx) = refs[34:43]
    (val_tx, val_rx, proj_tx, proj_rx, spread_tx, proj_all, sq2_tx, sq2_rx) = refs[43:51]
    (fin_tx, fin, tmp, load_sem, send_sem, recv_sem) = refs[51:57]
    tok_rows, inner_width = inner.shape
    rows = tok_rows * peers
    slab = inner_width // peers
    state = bc.shape[1] // 2
    total_heads = heads * peers
    me = lax.axis_index("tok")
    order = [peers // 2]
    for d in range(1, peers // 2):
        order += [peers // 2 - d, peers // 2 + d]

    def peer(d):
        return lax.rem(me + d, peers)

    def at(index, size):
        return pl.ds(pl.multiple_of(index * size, size), size)

    flights = []

    chips, core = (peers // 2, lax.rem(me, 2))
    chip = lax.div(me, 2)
    partner = me + 1 - 2 * core
    hops = sorted(range(1, chips), key=lambda k: -min(k, chips - k))

    def send(kind, d, src, dst, target=None):
        copy = pltpu.make_async_remote_copy(
            src_ref=src,
            dst_ref=dst,
            send_sem=send_sem.at[kind, d],
            recv_sem=recv_sem.at[kind, d],
            device_id={"tok": peer(d) if target is None else target},
            device_id_type=MESH,
        )
        copy.start()
        flights.append(copy)
        return copy

    mine = at(me, slab)
    my_rows = at(me, tok_rows)
    loads = [
        pltpu.make_async_copy(source, target, load_sem.at[index])
        for index, (source, target) in enumerate(
            [
                (raw, raw_all.at[my_rows, :]),
                (bc, bc_all.at[my_rows, :]),
                (inner.at[:, mine], inner_all.at[my_rows, :]),
                (gate.at[:, mine], gate_all.at[my_rows, :]),
                (residual.at[:, mine], res_all.at[my_rows, :]),
                *zip(small_hbm, small),
            ]
        )
    ]
    for load in loads:
        load.start()
    barrier = pltpu.get_barrier_semaphore()
    for d in range(1, peers):
        pl.semaphore_signal(barrier, inc=1, device_id={"tok": peer(d)}, device_id_type=MESH)
    pl.semaphore_wait(barrier, peers - 1)

    first = {}
    for d in order:
        first[RAW_K, d] = send(RAW_K, d, raw, raw_all.at[my_rows, :])
        first[BC_K, d] = send(BC_K, d, bc, bc_all.at[my_rows, :])
        first[INNER_K, d] = send(
            INNER_K, d, inner.at[:, at(peer(d), slab)], inner_all.at[my_rows, :]
        )
    for d in order:
        first[GATE_K, d] = send(GATE_K, d, gate.at[:, at(peer(d), slab)], gate_all.at[my_rows, :])
    for d in order:
        first[RES_K, d] = send(RES_K, d, residual.at[:, at(peer(d), slab)], res_all.at[my_rows, :])

    def exchange(kind, left, weights, tx, rx):
        def device(k, side):
            return 2 * lax.rem(chip + k, chips) + side

        def partial(index):
            return jnp.dot(left, weights[:, at(index, slab)], preferred_element_type=F32)

        halves, crossed = ({}, {})
        for k in hops + [0]:
            tx[k] = partial(device(k, 1 - core)).astype(BF)
            halves[k] = send(kind, k, tx.at[k], rx.at[k], partner)

        def joined(k):
            own = partial(device(k, core))
            halves[k].wait_recv()
            return own + rx[k].astype(F32)

        def forward(k):
            slot = chips + k
            tx[slot] = joined(k).astype(BF)
            crossed[slot] = send(kind, slot, tx.at[slot], rx.at[slot], device(k, core))

        def total():
            value = joined(0)
            for slot, copy in crossed.items():
                copy.wait_recv()
                value = value + rx[slot].astype(F32)
            return value

        return forward, total

    def arrived(copies, *kinds):
        for kind in kinds:
            for d in order:
                copies[kind, d].wait_recv()

    tmp[...] = jnp.zeros_like(tmp)
    for load in loads[5:11]:
        load.wait()
    for index, ref in enumerate((rate_one, bias_one, skip_one, rate_two, bias_two, skip_two)):
        tmp[index : index + 1, 0:total_heads] = ref[...]
    lanes = tmp.shape[1]
    turn = lax.rem(lanes - me * heads, lanes)
    params = pltpu.roll(tmp[...], turn, 1).T
    tmp[...] = jnp.zeros_like(tmp)
    loads[0].wait()
    arrived(first, RAW_K)
    tmp[:, 0:total_heads] = raw_all[...]
    steps = softplus(pltpu.roll(tmp[...], turn, 1).T[0:8] + params[0:8, 1:2])
    loads[1].wait()
    loads[2].wait()
    arrived(first, BC_K, INNER_K)
    scanned = ssd_heads(
        inner_all[...],
        bc_all[:, 0:state],
        bc_all[:, state : 2 * state],
        steps,
        params[0:8, 0:1],
        params[0:8, 2:3],
        heads,
        tmp,
    )
    loads[3].wait()
    arrived(first, GATE_K)
    gated = scanned * jax.nn.silu(gate_all[...].astype(F32))
    sq1_tx[...] = as_rows(jnp.sum(gated * gated, axis=1, keepdims=True))
    second = {}
    for d in order:
        second[SQ1_K, d] = send(SQ1_K, d, sq1_tx, sq1_rx.at[d])
    loads[11].wait()
    loads[12].wait()
    scaled = (gated * norm_gain[:, mine]).astype(BF)
    forward, total = exchange(OUT_K, scaled, out_w, out_tx, out_rx)
    for k in hops:
        forward(k)
    loads[4].wait()
    arrived(first, RES_K)
    arrived(second, SQ1_K)
    squares = sq1_tx[...]
    for d in order:
        squares = squares + sq1_rx[d]
    scale = as_column(lax.rsqrt(squares[0:1] / inner_width + 1e-05))
    hidden = (res_all[...].astype(F32) + scale * total()).astype(BF)
    to = lax.broadcasted_iota(jnp.int32, (rows, rows), 0)
    raster = lax.broadcasted_iota(jnp.int32, (rows, rows), 1)
    moved = (raster % peers) * (rows // peers) + raster // peers
    hidden = jnp.dot((to == moved).astype(BF), hidden, preferred_element_type=F32)

    width = in_w.shape[1]
    for load in loads[13:19]:
        load.wait()
    pre = (hidden * pre_gain[:, mine]).astype(BF)
    logits = lax.dot_general(
        step_weight[:, mine], pre, (((1,), (1,)), ((), ())), preferred_element_type=F32
    )
    squares = as_rows(jnp.sum(hidden * hidden, axis=1, keepdims=True))
    for p in range(peers):
        sq2_tx[p, 0:heads, :] = logits[p * heads : (p + 1) * heads]
        sq2_tx[p, heads:8, :] = squares[heads:8]
    third = {}
    for d in order:
        third[SQ2_K, d] = send(SQ2_K, d, sq2_tx.at[peer(d)], sq2_rx.at[d])
    proj_tx[...] = jnp.dot(
        pre, in_w[:, inner_width:width], preferred_element_type=F32
    ).astype(BF)
    for d in order:
        third[PROJ_K, d] = send(
            PROJ_K, d, proj_tx.at[at(peer(d), tok_rows), :], proj_rx.at[d]
        )

    forward, total = exchange(VAL_K, pre, in_w, val_tx, val_rx)
    for k in hops[:1]:
        forward(k)
    proj = proj_tx[my_rows, :].astype(F32)
    for d in order:
        third[PROJ_K, d].wait_recv()
        proj = proj + proj_rx[d].astype(F32)
    spread_tx[...] = proj.astype(BF)
    for d in order:
        third[SPREAD_K, d] = send(SPREAD_K, d, spread_tx, proj_all.at[my_rows, :])
    proj_all[my_rows, :] = spread_tx[...]
    for k in hops[1:]:
        forward(k)
    arrived(third, SQ2_K)
    gathered = sq2_tx[me]
    for d in order:
        gathered = gathered + sq2_rx[d]
    scale_row = lax.rsqrt(gathered[heads : heads + 1] / inner_width + 1e-05)
    scale = as_column(scale_row)
    steps = softplus(scale_row * gathered + params[0:8, 4:5])

    def convolve(projected, columns):
        taps = conv_weight[:, columns].astype(F32)
        place = lax.broadcasted_iota(jnp.int32, projected.shape, 0)
        mixed = conv_bias[:, columns]
        for offset in range(KC):
            back = KC - 1 - offset
            term = projected
            if back:
                term = jnp.where(place < back, 0.0, pltpu.roll(projected, back, 0))
            mixed = mixed + taps[offset : offset + 1] * term
        return jax.nn.silu(mixed).astype(BF)

    arrived(third, SPREAD_K)
    both = convolve(scale * proj_all[...].astype(F32), slice(inner_width, width))
    scanned = ssd_heads(
        convolve(scale * total(), mine),
        both[:, 0:state],
        both[:, state : 2 * state],
        steps,
        params[0:8, 3:4],
        params[0:8, 5:6],
        heads,
        tmp,
    ).astype(BF)
    fin_tx[...] = scanned
    last = {}
    for d in order:
        last[FIN_K, d] = send(FIN_K, d, fin_tx.at[at(peer(d), tok_rows), :], fin.at[:, mine])
    fin[:, mine] = fin_tx[my_rows, :]
    arrived(last, FIN_K)
    result[...] = rms_scale(fin[...].astype(F32), final_gain[0]).astype(BF)
    for copy in flights:
        copy.wait_send()


def fused_local(peers, *args):
    (inner, gate, bc, raw, rate_one, bias_one, skip_one, norm_gain, out_w, residual) = args[:10]
    (pre_gain, in_w, conv_w, conv_bias, step_w, bias_two, rate_two, skip_two, final_gain) = args[10:]
    tok_rows, inner_width = inner.shape
    heads = rate_one.shape[0] // peers
    rows, slab = (tok_rows * peers, inner_width // peers)
    state2 = bc.shape[1]

    def flat(vector):
        return vector.reshape(1, vector.shape[0])

    big = (inner, gate, bc, raw, residual)
    small = tuple(map(flat, (rate_one, bias_one, skip_one, rate_two, bias_two, skip_two)))
    small += (out_w, flat(norm_gain), flat(pre_gain), in_w, step_w.T, conv_w)
    small += (flat(conv_bias), flat(final_gain))
    block = pltpu.VMEM((rows, slab), BF)
    blocks = pltpu.VMEM((peers, rows, slab), BF)
    tiles = pltpu.VMEM((peers, 8, rows), F32)
    sends = pltpu.SemaphoreType.DMA((KINDS, peers))
    return pl.pallas_call(
        functools.partial(fused, peers, heads),
        out_shape=jax.ShapeDtypeStruct((tok_rows, inner_width), BF),
        in_specs=[pl.BlockSpec(memory_space=pltpu.HBM)] * (len(big) + len(small)),
        out_specs=pl.BlockSpec(memory_space=pltpu.VMEM),
        scratch_shapes=[pltpu.VMEM(part.shape, part.dtype) for part in small]
        + [
            block,
            block,
            pltpu.VMEM((rows, state2), BF),
            pltpu.VMEM((rows, raw.shape[1]), F32),
            block,
            blocks,
            blocks,
            pltpu.VMEM((8, rows), F32),
            tiles,
            blocks,
            blocks,
            pltpu.VMEM((rows, state2), BF),
            pltpu.VMEM((peers, tok_rows, state2), BF),
            pltpu.VMEM((tok_rows, state2), BF),
            pltpu.VMEM((rows, state2), BF),
            tiles,
            tiles,
            block,
            pltpu.VMEM((tok_rows, inner_width), BF),
            pltpu.VMEM((rows, rows), F32),
            pltpu.SemaphoreType.DMA((LOADS,)),
            sends,
            sends,
        ],
        compiler_params=pltpu.CompilerParams(
            collective_id=0, has_side_effects=True, vmem_limit_bytes=60 * 1024 * 1024
        ),
    )(*big, *small)


def local_step(peers, *args):
    inner, bc, rates = (args[0], args[2], args[4])
    tok_rows, inner_width = inner.shape
    heads = rates.shape[0]
    fits = (
        tok_rows * peers == 128
        and peers % 2 == 0
        and tok_rows % 16 == 0
        and tok_rows % peers == 0
        and heads % peers == 0
        and heads // peers < 8
        and heads <= 128
        and inner_width % (128 * peers) == 0
        and args[9].shape[1] == inner_width
        and bc.shape[1] == 256
    )
    return fused_local(peers, *args) if fits else local(*args)


def solution(mesh):
    placed = (
        P(("batch", "tok"), None),
        P(("batch", "tok"), None),
        P(("batch", "tok"), None),
        P(("batch", "tok"), None),
        P(),
        P(),
        P(),
        P(),
        P("tok", None),
        P(("batch", "tok"), None),
        P(),
        P("tok", None),
        P(),
        P(),
        P(),
        P(),
        P(),
        P(),
        P(),
    )
    return jax.shard_map(
        functools.partial(local_step, mesh.shape["tok"]), mesh=mesh, in_specs=placed, out_specs=P(("batch", "tok"), None), check_vma=False
    )
```

```python
import functools

import jax
import jax.numpy as jnp
from jax import lax
from jax.experimental import pallas as pl
from jax.experimental.pallas import tpu as pltpu
from jax.sharding import PartitionSpec as P

KC = 4
COL_DEV = 1


def prefix(value, axis, combine, identity):
    peers, here = (lax.axis_size(axis), lax.axis_index(axis))
    everything = jax.tree.map(lambda part: lax.all_gather(part, axis), value)
    start = jax.tree.map(
        lambda part, zero: jnp.broadcast_to(jnp.asarray(zero, part.dtype), part.shape),
        value,
        identity,
    )

    def hop(k, before):
        reached = k < here
        new = combine(before, jax.tree.map(lambda part: part[k], everything))
        return jax.tree.map(lambda a, b: jnp.where(reached, a, b), new, before)

    return lax.fori_loop(0, peers, hop, start)


def shifted(value, axis, steps):
    count = lax.axis_size(axis)
    first, last = (max(0, -steps), min(count, count - steps))
    return lax.ppermute(value, axis, [(source, source + steps) for source in range(first, last)])


def chain_join(earlier, following):
    early_decay, early_state = earlier
    late_decay, late_state = following
    return (early_decay + late_decay, jnp.exp(late_decay)[:, None, None] * early_state + late_state)


def advance(entering, scan_item):
    block_decay, block_state = scan_item
    return (jnp.exp(block_decay)[:, None, None] * entering + block_state, entering)


def rms_scale(matrix, gains):
    return (
        matrix
        * lax.rsqrt(jnp.mean(matrix * matrix, axis=-1, keepdims=True) + 1e-05)
        * gains[None, :]
    )


def entering_state(device_decay, local_final):
    heads, state_width, head_width = local_final.shape
    zero_state = jnp.zeros((heads, state_width, head_width), jnp.float32)
    ignored, incoming = prefix(
        (device_decay, local_final),
        "tok",
        chain_join,
        (jnp.zeros((heads,), jnp.float32), zero_state),
    )
    return incoming


def ssd_local(values, write_side, read_side, steps, rates, skips):
    tok_rows = values.shape[0]
    heads = rates.shape[0]
    head_width = values.shape[1] // heads
    state_width = write_side.shape[1]
    block_len = min(256, tok_rows)
    blocks = tok_rows // block_len
    step_blocks = steps.reshape(blocks, block_len, heads)
    cumulative = jnp.cumsum(-rates[None, None, :] * step_blocks, axis=1)
    value_blocks = values.reshape(blocks, block_len, heads, head_width)
    write_blocks = write_side.reshape(blocks, block_len, state_width)
    read_blocks = read_side.reshape(blocks, block_len, state_width)
    write_scale = jnp.exp(cumulative[:, -1:, :] - cumulative) * step_blocks
    written = (write_blocks[:, :, None, :].astype(jnp.float32) * write_scale[:, :, :, None]).astype(
        jnp.bfloat16
    )
    block_states = jnp.einsum(
        "bqhn,bqhp->bhnp", written, value_blocks, preferred_element_type=jnp.float32
    )
    block_decay = cumulative[:, -1, :]
    zero_state = jnp.zeros((heads, state_width, head_width), jnp.float32)
    local_final, local_entry = lax.scan(advance, zero_state, (block_decay, block_states))
    device_decay = jnp.sum(block_decay, axis=0)
    incoming = entering_state(device_decay, local_final)
    decay_before = jnp.cumsum(block_decay, axis=0) - block_decay
    entry = local_entry + jnp.exp(decay_before)[:, :, None, None] * incoming[None]
    intersections = jnp.einsum(
        "btn,bsn->bts", read_blocks, write_blocks, preferred_element_type=jnp.float32
    )
    by_head = jnp.transpose(cumulative, (0, 2, 1))
    lower_mask = jnp.tril(jnp.ones((block_len, block_len), bool))
    decay = jnp.exp(
        jnp.where(lower_mask[None, None], by_head[:, :, :, None] - by_head[:, :, None, :], -jnp.inf)
    )
    step_heads = jnp.transpose(step_blocks, (0, 2, 1))
    mixing = (intersections[:, None] * decay * step_heads[:, :, None, :]).astype(jnp.bfloat16)
    diagonal = jnp.einsum(
        "bhts,bshp->bthp", mixing, value_blocks, preferred_element_type=jnp.float32
    )
    carried = (
        jnp.einsum(
            "btn,bhnp->bthp",
            read_blocks.astype(jnp.float32),
            entry,
            precision=lax.Precision.HIGHEST,
        )
        * jnp.exp(cumulative)[:, :, :, None]
    )
    result = diagonal + carried + skips[None, None, :, None] * value_blocks.astype(jnp.float32)
    return result.reshape(tok_rows, heads * head_width)


def local(
    inner_first,
    gate_first,
    bc_first,
    first_raw_steps,
    rate_first,
    bias_first,
    skip_first,
    norm_gain,
    out_weight,
    residual,
    pre_gain,
    in_weight,
    conv_weight,
    conv_bias,
    step_weight,
    bias_second,
    rate_second,
    skip_second,
    final_gain,
):
    state_width = bc_first.shape[1] // 2
    inner_width = inner_first.shape[1]
    model_width = residual.shape[1]
    out_whole, in_whole = (
        lax.all_gather(out_weight, "tok", axis=0, tiled=True),
        lax.all_gather(in_weight, "tok", axis=0, tiled=True),
    )
    steps_one = jax.nn.softplus(first_raw_steps + bias_first[None, :])
    scanned_one = ssd_local(
        inner_first,
        bc_first[:, :state_width],
        bc_first[:, state_width:],
        steps_one,
        rate_first,
        skip_first,
    )
    gated = scanned_one * jax.nn.silu(gate_first.astype(jnp.float32))
    normed_one = rms_scale(gated, norm_gain).astype(jnp.bfloat16)
    hidden_raster = (
        residual.astype(jnp.float32)
        + jnp.dot(normed_one, out_whole, preferred_element_type=jnp.float32)
    ).astype(jnp.bfloat16)
    tok_rows = hidden_raster.shape[0]
    peers = lax.axis_size("tok")
    raster_rows = tok_rows // (peers * COL_DEV)
    outgoing = hidden_raster.reshape(raster_rows, peers, COL_DEV, model_width).transpose(2, 1, 0, 3)
    arrived = lax.all_to_all(outgoing, "tok", split_axis=1, concat_axis=1, tiled=True)
    hidden_column = arrived.reshape(tok_rows, model_width)
    pre_normed = rms_scale(hidden_column.astype(jnp.float32), pre_gain).astype(jnp.bfloat16)
    rim_width = KC - 1
    projected = jnp.dot(pre_normed, in_whole, preferred_element_type=jnp.float32).astype(
        jnp.bfloat16
    )
    rim_projected = shifted(projected[tok_rows - rim_width :], "tok", 1)
    padded = jnp.concatenate([rim_projected, projected], axis=0)
    summed = conv_bias[None, :]
    for offset in range(KC):
        summed = (
            summed
            + conv_weight[offset].astype(jnp.float32)[None, :] * padded[offset : offset + tok_rows]
        )
    convolved = jax.nn.silu(summed).astype(jnp.bfloat16)
    steps_two = jax.nn.softplus(
        jnp.dot(pre_normed, step_weight, preferred_element_type=jnp.float32) + bias_second[None, :]
    )
    scanned_two = ssd_local(
        convolved[:, :inner_width],
        convolved[:, inner_width : inner_width + state_width],
        convolved[:, inner_width + state_width :],
        steps_two,
        rate_second,
        skip_second,
    )
    return rms_scale(scanned_two, final_gain).astype(jnp.bfloat16)


MESH = pl.DeviceIdType.MESH
BF = jnp.bfloat16
F32 = jnp.float32
INNER_K, BC_K, RAW_K, GATE_K, RES_K, SQ1_K, OUT_K, SQ2_K, VAL_K, PROJ_K, SPREAD_K, FIN_K = range(12)
KINDS = 12
LOADS = 19


def softplus(x):
    return jnp.maximum(x, 0.0) + jnp.log1p(jnp.exp(-jnp.abs(x)))


def as_column(row):
    rows = row.shape[1]
    return jnp.broadcast_to(row, (rows, rows)).T[:, 0:1]


def as_rows(column):
    rows = column.shape[0]
    return jnp.broadcast_to(column, (rows, rows)).T[0:8]


def mixweights(write_side, read_side, steps, rates, heads, tmp):
    rows = write_side.shape[0]
    at = lax.broadcasted_iota(jnp.int32, (rows, rows), 0)
    source = lax.broadcasted_iota(jnp.int32, (rows, rows), 1)
    ahead = (at <= source).astype(F32)
    cumulative = jnp.dot(
        -rates * steps, ahead, precision=lax.Precision.HIGHEST, preferred_element_type=F32
    )
    tmp[0:8, :] = cumulative
    columns = tmp[...].T
    scores = lax.dot_general(
        read_side, write_side, (((1,), (1,)), ((), ())), preferred_element_type=F32
    )
    lower = source <= at
    mixing = []
    for h in range(heads):
        gap = columns[:, h : h + 1] - cumulative[h : h + 1, :]
        decay = jnp.exp(jnp.where(lower, gap, -1e30))
        mixing.append((scores * decay * steps[h : h + 1, :]).astype(BF))
    return jnp.concatenate(mixing, axis=0)


def apply_mix(mixing, values, skips, heads):
    rows, width = values.shape
    head = width // heads
    product = jnp.dot(mixing, values, preferred_element_type=F32)
    owner = lax.broadcasted_iota(jnp.int32, (rows, width), 1) // head
    wide = values.astype(F32)
    result = jnp.zeros((rows, width), F32)
    for h in range(heads):
        part = product[h * rows : (h + 1) * rows] + skips[h : h + 1, :] * wide
        result = jnp.where(owner == h, part, result)
    return result


def fused(peers, heads, *refs):
    (inner, gate, bc, raw), (residual,), small_hbm = (refs[0:4], refs[4:5], refs[5:19])
    result, small = (refs[19], refs[20:34])
    (rate_one, bias_one, skip_one, rate_two, bias_two, skip_two) = small[0:6]
    (out_w, norm_gain, pre_gain, in_w, step_weight, conv_weight, conv_bias, final_gain) = small[6:14]
    (inner_all, gate_all, bc_all, raw_all, res_all, out_tx, out_rx, sq1_tx, sq1_rx) = refs[34:43]
    (val_tx, val_rx, proj_tx, proj_rx, spread_tx, proj_all, sq2_tx, sq2_rx) = refs[43:51]
    (fin_tx, fin, tmp, mixing_ref, load_sem, send_sem, recv_sem) = refs[51:58]
    tok_rows, inner_width = inner.shape
    rows = tok_rows * peers
    slab = inner_width // peers
    state = bc.shape[1] // 2
    total_heads = heads * peers
    me = lax.axis_index("tok")
    order = [peers // 2]
    for d in range(1, peers // 2):
        order += [peers // 2 - d, peers // 2 + d]

    def peer(d):
        return lax.rem(me + d, peers)

    def at(index, size):
        return pl.ds(pl.multiple_of(index * size, size), size)

    flights = []

    chips, core = (peers // 2, lax.rem(me, 2))
    chip = lax.div(me, 2)
    partner = me + 1 - 2 * core
    hops = sorted(range(1, chips), key=lambda k: -min(k, chips - k))

    def send(kind, d, src, dst, target=None):
        copy = pltpu.make_async_remote_copy(
            src_ref=src,
            dst_ref=dst,
            send_sem=send_sem.at[kind, d],
            recv_sem=recv_sem.at[kind, d],
            device_id={"tok": peer(d) if target is None else target},
            device_id_type=MESH,
        )
        copy.start()
        flights.append(copy)
        return copy

    mine = at(me, slab)
    my_rows = at(me, tok_rows)
    loads = [
        pltpu.make_async_copy(source, target, load_sem.at[index])
        for index, (source, target) in enumerate(
            [
                (raw, raw_all.at[my_rows, :]),
                (bc, bc_all.at[my_rows, :]),
                (inner.at[:, mine], inner_all.at[my_rows, :]),
                (gate.at[:, mine], gate_all.at[my_rows, :]),
                (residual.at[:, mine], res_all.at[my_rows, :]),
                *zip(small_hbm, small),
            ]
        )
    ]
    for load in loads:
        load.start()
    barrier = pltpu.get_barrier_semaphore()
    for d in range(1, peers):
        pl.semaphore_signal(barrier, inc=1, device_id={"tok": peer(d)}, device_id_type=MESH)
    pl.semaphore_wait(barrier, peers - 1)

    first = {}
    for d in order:
        first[RAW_K, d] = send(RAW_K, d, raw, raw_all.at[my_rows, :])
        first[BC_K, d] = send(BC_K, d, bc, bc_all.at[my_rows, :])
        first[INNER_K, d] = send(
            INNER_K, d, inner.at[:, at(peer(d), slab)], inner_all.at[my_rows, :]
        )
    for d in order:
        first[GATE_K, d] = send(GATE_K, d, gate.at[:, at(peer(d), slab)], gate_all.at[my_rows, :])
    for d in order:
        first[RES_K, d] = send(RES_K, d, residual.at[:, at(peer(d), slab)], res_all.at[my_rows, :])

    def exchange(kind, left, weights, tx, rx):
        def device(k, side):
            return 2 * lax.rem(chip + k, chips) + side

        def partial(index):
            return jnp.dot(left, weights[:, at(index, slab)], preferred_element_type=F32)

        halves, crossed = ({}, {})
        for k in hops + [0]:
            tx[k] = partial(device(k, 1 - core)).astype(BF)
            halves[k] = send(kind, k, tx.at[k], rx.at[k], partner)

        def joined(k):
            own = partial(device(k, core))
            halves[k].wait_recv()
            return own + rx[k].astype(F32)

        def forward(k):
            slot = chips + k
            tx[slot] = joined(k).astype(BF)
            crossed[slot] = send(kind, slot, tx.at[slot], rx.at[slot], device(k, core))

        def total():
            value = joined(0)
            for slot, copy in crossed.items():
                copy.wait_recv()
                value = value + rx[slot].astype(F32)
            return value

        return forward, total

    def arrived(copies, *kinds):
        for kind in kinds:
            for d in order:
                copies[kind, d].wait_recv()

    tmp[...] = jnp.zeros_like(tmp)
    for load in loads[5:11]:
        load.wait()
    for index, ref in enumerate((rate_one, bias_one, skip_one, rate_two, bias_two, skip_two)):
        tmp[index : index + 1, 0:total_heads] = ref[...]
    lanes = tmp.shape[1]
    turn = lax.rem(lanes - me * heads, lanes)
    params = pltpu.roll(tmp[...], turn, 1).T
    tmp[...] = jnp.zeros_like(tmp)
    loads[0].wait()
    arrived(first, RAW_K)
    tmp[:, 0:total_heads] = raw_all[...]
    steps = softplus(pltpu.roll(tmp[...], turn, 1).T[0:8] + params[0:8, 1:2])
    loads[1].wait()
    arrived(first, BC_K)
    mixing_ref[...] = mixweights(
        bc_all[:, 0:state], bc_all[:, state : 2 * state], steps, params[0:8, 0:1], heads, tmp
    )
    loads[2].wait()
    arrived(first, INNER_K)
    scanned = apply_mix(mixing_ref[...], inner_all[...], params[0:8, 2:3], heads)
    loads[3].wait()
    arrived(first, GATE_K)
    gated = scanned * jax.nn.silu(gate_all[...].astype(F32))
    sq1_tx[...] = as_rows(jnp.sum(gated * gated, axis=1, keepdims=True))
    second = {}
    for d in order:
        second[SQ1_K, d] = send(SQ1_K, d, sq1_tx, sq1_rx.at[d])
    loads[11].wait()
    loads[12].wait()
    scaled = (gated * norm_gain[:, mine]).astype(BF)
    forward, total = exchange(OUT_K, scaled, out_w, out_tx, out_rx)
    for k in hops:
        forward(k)
    loads[4].wait()
    arrived(first, RES_K)
    arrived(second, SQ1_K)
    squares = sq1_tx[...]
    for d in order:
        squares = squares + sq1_rx[d]
    scale = as_column(lax.rsqrt(squares[0:1] / inner_width + 1e-05))
    hidden = (res_all[...].astype(F32) + scale * total()).astype(BF)
    to = lax.broadcasted_iota(jnp.int32, (rows, rows), 0)
    raster = lax.broadcasted_iota(jnp.int32, (rows, rows), 1)
    moved = (raster % peers) * (rows // peers) + raster // peers
    hidden = jnp.dot((to == moved).astype(BF), hidden, preferred_element_type=F32)

    width = in_w.shape[1]
    for load in loads[13:19]:
        load.wait()
    pre = (hidden * pre_gain[:, mine]).astype(BF)
    logits = lax.dot_general(
        step_weight[:, mine], pre, (((1,), (1,)), ((), ())), preferred_element_type=F32
    )
    squares = as_rows(jnp.sum(hidden * hidden, axis=1, keepdims=True))
    for p in range(peers):
        sq2_tx[p, 0:heads, :] = logits[p * heads : (p + 1) * heads]
        sq2_tx[p, heads:8, :] = squares[heads:8]
    third = {}
    for d in order:
        third[SQ2_K, d] = send(SQ2_K, d, sq2_tx.at[peer(d)], sq2_rx.at[d])
    proj_tx[...] = jnp.dot(
        pre, in_w[:, inner_width:width], preferred_element_type=F32
    ).astype(BF)
    for d in order:
        third[PROJ_K, d] = send(
            PROJ_K, d, proj_tx.at[at(peer(d), tok_rows), :], proj_rx.at[d]
        )

    forward, total = exchange(VAL_K, pre, in_w, val_tx, val_rx)
    for k in hops[:1]:
        forward(k)
    proj = proj_tx[my_rows, :].astype(F32)
    for d in order:
        third[PROJ_K, d].wait_recv()
        proj = proj + proj_rx[d].astype(F32)
    spread_tx[...] = proj.astype(BF)
    for d in order:
        third[SPREAD_K, d] = send(SPREAD_K, d, spread_tx, proj_all.at[my_rows, :])
    proj_all[my_rows, :] = spread_tx[...]
    for k in hops[1:]:
        forward(k)
    arrived(third, SQ2_K)
    gathered = sq2_tx[me]
    for d in order:
        gathered = gathered + sq2_rx[d]
    scale_row = lax.rsqrt(gathered[heads : heads + 1] / inner_width + 1e-05)
    scale = as_column(scale_row)
    steps = softplus(scale_row * gathered + params[0:8, 4:5])

    def bias_row(start, size):
        pieces = [conv_bias[pl.ds(start + i, 1), :] for i in range(size // 128)]
        return jnp.concatenate(pieces, axis=1)

    def convolve(projected, columns, bias):
        taps = conv_weight[:, columns].astype(F32)
        place = lax.broadcasted_iota(jnp.int32, projected.shape, 0)
        mixed = bias
        for offset in range(KC):
            back = KC - 1 - offset
            term = projected
            if back:
                term = jnp.where(place < back, 0.0, pltpu.roll(projected, back, 0))
            mixed = mixed + taps[offset : offset + 1] * term
        return jax.nn.silu(mixed).astype(BF)

    arrived(third, SPREAD_K)
    both = convolve(scale * proj_all[...].astype(F32), slice(inner_width, width), bias_row(inner_width // 128, width - inner_width))
    mixing_ref[...] = mixweights(
        both[:, 0:state], both[:, state : 2 * state], steps, params[0:8, 3:4], heads, tmp
    )
    values = convolve(scale * total(), mine, bias_row(me * (slab // 128), slab))
    scanned = apply_mix(mixing_ref[...], values, params[0:8, 5:6], heads).astype(BF)
    fin_tx[...] = scanned
    last = {}
    for d in order:
        last[FIN_K, d] = send(FIN_K, d, fin_tx.at[at(peer(d), tok_rows), :], fin.at[:, mine])
    fin[:, mine] = fin_tx[my_rows, :]
    arrived(last, FIN_K)
    result[...] = rms_scale(fin[...].astype(F32), final_gain[0]).astype(BF)
    for copy in flights:
        copy.wait_send()


def fused_local(peers, *args):
    (inner, gate, bc, raw, rate_one, bias_one, skip_one, norm_gain, out_w, residual) = args[:10]
    (pre_gain, in_w, conv_w, conv_bias, step_w, bias_two, rate_two, skip_two, final_gain) = args[10:]
    tok_rows, inner_width = inner.shape
    heads = rate_one.shape[0] // peers
    rows, slab = (tok_rows * peers, inner_width // peers)
    state2 = bc.shape[1]

    def flat(vector):
        return vector.reshape(1, vector.shape[0])

    big = (inner, gate, bc, raw, residual)
    small = tuple(map(flat, (rate_one, bias_one, skip_one, rate_two, bias_two, skip_two)))
    small += (out_w, flat(norm_gain), flat(pre_gain), in_w, step_w.T, conv_w)
    small += (conv_bias.reshape(-1, 128), flat(final_gain))
    block = pltpu.VMEM((rows, slab), BF)
    blocks = pltpu.VMEM((peers, rows, slab), BF)
    tiles = pltpu.VMEM((peers, 8, rows), F32)
    sends = pltpu.SemaphoreType.DMA((KINDS, peers))
    return pl.pallas_call(
        functools.partial(fused, peers, heads),
        out_shape=jax.ShapeDtypeStruct((tok_rows, inner_width), BF),
        in_specs=[pl.BlockSpec(memory_space=pltpu.HBM)] * (len(big) + len(small)),
        out_specs=pl.BlockSpec(memory_space=pltpu.VMEM),
        scratch_shapes=[pltpu.VMEM(part.shape, part.dtype) for part in small]
        + [
            block,
            block,
            pltpu.VMEM((rows, state2), BF),
            pltpu.VMEM((rows, raw.shape[1]), F32),
            block,
            blocks,
            blocks,
            pltpu.VMEM((8, rows), F32),
            tiles,
            blocks,
            blocks,
            pltpu.VMEM((rows, state2), BF),
            pltpu.VMEM((peers, tok_rows, state2), BF),
            pltpu.VMEM((tok_rows, state2), BF),
            pltpu.VMEM((rows, state2), BF),
            tiles,
            tiles,
            block,
            pltpu.VMEM((tok_rows, inner_width), BF),
            pltpu.VMEM((rows, rows), F32),
            pltpu.VMEM((heads * rows, rows), BF),
            pltpu.SemaphoreType.DMA((LOADS,)),
            sends,
            sends,
        ],
        compiler_params=pltpu.CompilerParams(
            collective_id=0, has_side_effects=True, vmem_limit_bytes=60 * 1024 * 1024
        ),
    )(*big, *small)


def local_step(peers, *args):
    inner, bc, rates = (args[0], args[2], args[4])
    tok_rows, inner_width = inner.shape
    heads = rates.shape[0]
    fits = (
        tok_rows * peers == 128
        and peers % 2 == 0
        and tok_rows % 16 == 0
        and tok_rows % peers == 0
        and heads % peers == 0
        and heads // peers < 8
        and heads <= 128
        and inner_width % (128 * peers) == 0
        and args[9].shape[1] == inner_width
        and bc.shape[1] == 256
    )
    return fused_local(peers, *args) if fits else local(*args)


def solution(mesh):
    placed = (
        P(("batch", "tok"), None),
        P(("batch", "tok"), None),
        P(("batch", "tok"), None),
        P(("batch", "tok"), None),
        P(),
        P(),
        P(),
        P(),
        P("tok", None),
        P(("batch", "tok"), None),
        P(),
        P("tok", None),
        P(),
        P(),
        P(),
        P(),
        P(),
        P(),
        P(),
    )
    return jax.shard_map(
        functools.partial(local_step, mesh.shape["tok"]), mesh=mesh, in_specs=placed, out_specs=P(("batch", "tok"), None), check_vma=False
    )
```

```python
import functools

import jax
import jax.numpy as jnp
from jax import lax
from jax.experimental import pallas as pl
from jax.experimental.pallas import tpu as pltpu
from jax.sharding import PartitionSpec as P

KC = 4
COL_DEV = 1


def prefix(value, axis, combine, identity):
    peers, here = (lax.axis_size(axis), lax.axis_index(axis))
    everything = jax.tree.map(lambda part: lax.all_gather(part, axis), value)
    start = jax.tree.map(
        lambda part, zero: jnp.broadcast_to(jnp.asarray(zero, part.dtype), part.shape),
        value,
        identity,
    )

    def hop(k, before):
        reached = k < here
        new = combine(before, jax.tree.map(lambda part: part[k], everything))
        return jax.tree.map(lambda a, b: jnp.where(reached, a, b), new, before)

    return lax.fori_loop(0, peers, hop, start)


def shifted(value, axis, steps):
    count = lax.axis_size(axis)
    first, last = (max(0, -steps), min(count, count - steps))
    return lax.ppermute(value, axis, [(source, source + steps) for source in range(first, last)])


def chain_join(earlier, following):
    early_decay, early_state = earlier
    late_decay, late_state = following
    return (early_decay + late_decay, jnp.exp(late_decay)[:, None, None] * early_state + late_state)


def advance(entering, scan_item):
    block_decay, block_state = scan_item
    return (jnp.exp(block_decay)[:, None, None] * entering + block_state, entering)


def rms_scale(matrix, gains):
    return (
        matrix
        * lax.rsqrt(jnp.mean(matrix * matrix, axis=-1, keepdims=True) + 1e-05)
        * gains[None, :]
    )


def entering_state(device_decay, local_final):
    heads, state_width, head_width = local_final.shape
    zero_state = jnp.zeros((heads, state_width, head_width), jnp.float32)
    ignored, incoming = prefix(
        (device_decay, local_final),
        "tok",
        chain_join,
        (jnp.zeros((heads,), jnp.float32), zero_state),
    )
    return incoming


def ssd_local(values, write_side, read_side, steps, rates, skips):
    tok_rows = values.shape[0]
    heads = rates.shape[0]
    head_width = values.shape[1] // heads
    state_width = write_side.shape[1]
    block_len = min(256, tok_rows)
    blocks = tok_rows // block_len
    step_blocks = steps.reshape(blocks, block_len, heads)
    cumulative = jnp.cumsum(-rates[None, None, :] * step_blocks, axis=1)
    value_blocks = values.reshape(blocks, block_len, heads, head_width)
    write_blocks = write_side.reshape(blocks, block_len, state_width)
    read_blocks = read_side.reshape(blocks, block_len, state_width)
    write_scale = jnp.exp(cumulative[:, -1:, :] - cumulative) * step_blocks
    written = (write_blocks[:, :, None, :].astype(jnp.float32) * write_scale[:, :, :, None]).astype(
        jnp.bfloat16
    )
    block_states = jnp.einsum(
        "bqhn,bqhp->bhnp", written, value_blocks, preferred_element_type=jnp.float32
    )
    block_decay = cumulative[:, -1, :]
    zero_state = jnp.zeros((heads, state_width, head_width), jnp.float32)
    local_final, local_entry = lax.scan(advance, zero_state, (block_decay, block_states))
    device_decay = jnp.sum(block_decay, axis=0)
    incoming = entering_state(device_decay, local_final)
    decay_before = jnp.cumsum(block_decay, axis=0) - block_decay
    entry = local_entry + jnp.exp(decay_before)[:, :, None, None] * incoming[None]
    intersections = jnp.einsum(
        "btn,bsn->bts", read_blocks, write_blocks, preferred_element_type=jnp.float32
    )
    by_head = jnp.transpose(cumulative, (0, 2, 1))
    lower_mask = jnp.tril(jnp.ones((block_len, block_len), bool))
    decay = jnp.exp(
        jnp.where(lower_mask[None, None], by_head[:, :, :, None] - by_head[:, :, None, :], -jnp.inf)
    )
    step_heads = jnp.transpose(step_blocks, (0, 2, 1))
    mixing = (intersections[:, None] * decay * step_heads[:, :, None, :]).astype(jnp.bfloat16)
    diagonal = jnp.einsum(
        "bhts,bshp->bthp", mixing, value_blocks, preferred_element_type=jnp.float32
    )
    carried = (
        jnp.einsum(
            "btn,bhnp->bthp",
            read_blocks.astype(jnp.float32),
            entry,
            precision=lax.Precision.HIGHEST,
        )
        * jnp.exp(cumulative)[:, :, :, None]
    )
    result = diagonal + carried + skips[None, None, :, None] * value_blocks.astype(jnp.float32)
    return result.reshape(tok_rows, heads * head_width)


def local(
    inner_first,
    gate_first,
    bc_first,
    first_raw_steps,
    rate_first,
    bias_first,
    skip_first,
    norm_gain,
    out_weight,
    residual,
    pre_gain,
    in_weight,
    conv_weight,
    conv_bias,
    step_weight,
    bias_second,
    rate_second,
    skip_second,
    final_gain,
):
    state_width = bc_first.shape[1] // 2
    inner_width = inner_first.shape[1]
    model_width = residual.shape[1]
    out_whole, in_whole = (
        lax.all_gather(out_weight, "tok", axis=0, tiled=True),
        lax.all_gather(in_weight, "tok", axis=0, tiled=True),
    )
    steps_one = jax.nn.softplus(first_raw_steps + bias_first[None, :])
    scanned_one = ssd_local(
        inner_first,
        bc_first[:, :state_width],
        bc_first[:, state_width:],
        steps_one,
        rate_first,
        skip_first,
    )
    gated = scanned_one * jax.nn.silu(gate_first.astype(jnp.float32))
    normed_one = rms_scale(gated, norm_gain).astype(jnp.bfloat16)
    hidden_raster = (
        residual.astype(jnp.float32)
        + jnp.dot(normed_one, out_whole, preferred_element_type=jnp.float32)
    ).astype(jnp.bfloat16)
    tok_rows = hidden_raster.shape[0]
    peers = lax.axis_size("tok")
    raster_rows = tok_rows // (peers * COL_DEV)
    outgoing = hidden_raster.reshape(raster_rows, peers, COL_DEV, model_width).transpose(2, 1, 0, 3)
    arrived = lax.all_to_all(outgoing, "tok", split_axis=1, concat_axis=1, tiled=True)
    hidden_column = arrived.reshape(tok_rows, model_width)
    pre_normed = rms_scale(hidden_column.astype(jnp.float32), pre_gain).astype(jnp.bfloat16)
    rim_width = KC - 1
    projected = jnp.dot(pre_normed, in_whole, preferred_element_type=jnp.float32).astype(
        jnp.bfloat16
    )
    rim_projected = shifted(projected[tok_rows - rim_width :], "tok", 1)
    padded = jnp.concatenate([rim_projected, projected], axis=0)
    summed = conv_bias[None, :]
    for offset in range(KC):
        summed = (
            summed
            + conv_weight[offset].astype(jnp.float32)[None, :] * padded[offset : offset + tok_rows]
        )
    convolved = jax.nn.silu(summed).astype(jnp.bfloat16)
    steps_two = jax.nn.softplus(
        jnp.dot(pre_normed, step_weight, preferred_element_type=jnp.float32) + bias_second[None, :]
    )
    scanned_two = ssd_local(
        convolved[:, :inner_width],
        convolved[:, inner_width : inner_width + state_width],
        convolved[:, inner_width + state_width :],
        steps_two,
        rate_second,
        skip_second,
    )
    return rms_scale(scanned_two, final_gain).astype(jnp.bfloat16)


MESH = pl.DeviceIdType.MESH
BF = jnp.bfloat16
F32 = jnp.float32
INNER_K, BC_K, RAW_K, GATE_K, RES_K, SQ1_K, OUT_K, SQ2_K, VAL_K, PROJ_K, SPREAD_K, FIN_K = range(12)
KINDS = 12
LOADS = 19


def softplus(x):
    return jnp.maximum(x, 0.0) + jnp.log1p(jnp.exp(-jnp.abs(x)))


def as_column(row):
    rows = row.shape[1]
    return jnp.broadcast_to(row, (rows, rows)).T[:, 0:1]


def as_rows(column):
    rows = column.shape[0]
    return jnp.broadcast_to(column, (rows, rows)).T[0:8]


def mixweights(write_side, read_side, steps, rates, heads, tmp):
    rows = write_side.shape[0]
    at = lax.broadcasted_iota(jnp.int32, (rows, rows), 0)
    source = lax.broadcasted_iota(jnp.int32, (rows, rows), 1)
    ahead = (at <= source).astype(F32)
    cumulative = jnp.dot(
        -rates * steps, ahead, precision=lax.Precision.HIGHEST, preferred_element_type=F32
    )
    tmp[0:8, :] = cumulative
    columns = tmp[...].T
    scores = lax.dot_general(
        read_side, write_side, (((1,), (1,)), ((), ())), preferred_element_type=F32
    )
    lower = source <= at
    mixing = []
    for h in range(heads):
        gap = columns[:, h : h + 1] - cumulative[h : h + 1, :]
        decay = jnp.exp(jnp.where(lower, gap, -1e30))
        mixing.append((scores * decay * steps[h : h + 1, :]).astype(BF))
    return jnp.concatenate(mixing, axis=0)


def apply_mix(mixing, values, skips, heads):
    rows, width = values.shape
    head = width // heads
    product = jnp.dot(mixing, values, preferred_element_type=F32)
    owner = lax.broadcasted_iota(jnp.int32, (rows, width), 1) // head
    wide = values.astype(F32)
    result = jnp.zeros((rows, width), F32)
    for h in range(heads):
        part = product[h * rows : (h + 1) * rows] + skips[h : h + 1, :] * wide
        result = jnp.where(owner == h, part, result)
    return result


def fused(peers, heads, *refs):
    (inner, gate, bc, raw), (residual,), small_hbm = (refs[0:4], refs[4:5], refs[5:19])
    result, small = (refs[19], refs[20:34])
    (rate_one, bias_one, skip_one, rate_two, bias_two, skip_two) = small[0:6]
    (out_w, norm_gain, pre_gain, in_w, step_weight, conv_weight, conv_bias, final_gain) = small[6:14]
    (inner_all, gate_all, bc_all, raw_all, res_all, out_tx, out_rx, sq1_tx, sq1_rx) = refs[34:43]
    (val_tx, val_rx, proj_tx, proj_rx, spread_tx, proj_all, sq2_tx, sq2_rx) = refs[43:51]
    (fin_tx, fin, tmp, mixing_ref, load_sem, send_sem, recv_sem) = refs[51:58]
    tok_rows, inner_width = inner.shape
    rows = tok_rows * peers
    slab = inner_width // peers
    state = bc.shape[1] // 2
    total_heads = heads * peers
    me = lax.axis_index("tok")
    order = [peers // 2]
    for d in range(1, peers // 2):
        order += [peers // 2 - d, peers // 2 + d]

    def peer(d):
        return lax.rem(me + d, peers)

    def at(index, size):
        return pl.ds(pl.multiple_of(index * size, size), size)

    flights = []

    chips, core = (peers // 2, lax.rem(me, 2))
    chip = lax.div(me, 2)
    partner = me + 1 - 2 * core
    hops = sorted(range(1, chips), key=lambda k: -min(k, chips - k))

    def send(kind, d, src, dst, target=None):
        copy = pltpu.make_async_remote_copy(
            src_ref=src,
            dst_ref=dst,
            send_sem=send_sem.at[kind, d],
            recv_sem=recv_sem.at[kind, d],
            device_id={"tok": peer(d) if target is None else target},
            device_id_type=MESH,
        )
        copy.start()
        flights.append(copy)
        return copy

    mine = at(me, slab)
    my_rows = at(me, tok_rows)
    loads = [
        pltpu.make_async_copy(source, target, load_sem.at[index])
        for index, (source, target) in enumerate(
            [
                (raw, raw_all.at[my_rows, :]),
                (bc, bc_all.at[my_rows, :]),
                (inner.at[:, mine], inner_all.at[my_rows, :]),
                (gate.at[:, mine], gate_all.at[my_rows, :]),
                (residual.at[:, mine], res_all.at[my_rows, :]),
                *zip(small_hbm, small),
            ]
        )
    ]
    for load in loads:
        load.start()
    barrier = pltpu.get_barrier_semaphore()
    for d in range(1, peers):
        pl.semaphore_signal(barrier, inc=1, device_id={"tok": peer(d)}, device_id_type=MESH)
    pl.semaphore_wait(barrier, peers - 1)

    first = {}
    for d in order:
        first[RAW_K, d] = send(RAW_K, d, raw, raw_all.at[my_rows, :])
        first[BC_K, d] = send(BC_K, d, bc, bc_all.at[my_rows, :])
    for d in order:
        first[INNER_K, d] = send(
            INNER_K, d, inner.at[:, at(peer(d), slab)], inner_all.at[my_rows, :]
        )
    for d in order:
        first[GATE_K, d] = send(GATE_K, d, gate.at[:, at(peer(d), slab)], gate_all.at[my_rows, :])
    for d in order:
        first[RES_K, d] = send(RES_K, d, residual.at[:, at(peer(d), slab)], res_all.at[my_rows, :])

    def exchange(kind, left, weights, tx, rx):
        def device(k, side):
            return 2 * lax.rem(chip + k, chips) + side

        def partial(index):
            return jnp.dot(left, weights[:, at(index, slab)], preferred_element_type=F32)

        halves, crossed = ({}, {})
        for k in hops + [0]:
            tx[k] = partial(device(k, 1 - core)).astype(BF)
            halves[k] = send(kind, k, tx.at[k], rx.at[k], partner)

        def joined(k):
            own = partial(device(k, core))
            halves[k].wait_recv()
            return own + rx[k].astype(F32)

        def forward(k):
            slot = chips + k
            tx[slot] = joined(k).astype(BF)
            crossed[slot] = send(kind, slot, tx.at[slot], rx.at[slot], device(k, core))

        def total():
            value = joined(0)
            for slot, copy in crossed.items():
                copy.wait_recv()
                value = value + rx[slot].astype(F32)
            return value

        return forward, total

    def arrived(copies, *kinds):
        for kind in kinds:
            for d in order:
                copies[kind, d].wait_recv()

    tmp[...] = jnp.zeros_like(tmp)
    for load in loads[5:11]:
        load.wait()
    for index, ref in enumerate((rate_one, bias_one, skip_one, rate_two, bias_two, skip_two)):
        tmp[index : index + 1, 0:total_heads] = ref[...]
    lanes = tmp.shape[1]
    turn = lax.rem(lanes - me * heads, lanes)
    params = pltpu.roll(tmp[...], turn, 1).T
    tmp[...] = jnp.zeros_like(tmp)
    loads[0].wait()
    arrived(first, RAW_K)
    tmp[:, 0:total_heads] = raw_all[...]
    steps = softplus(pltpu.roll(tmp[...], turn, 1).T[0:8] + params[0:8, 1:2])
    loads[1].wait()
    arrived(first, BC_K)
    mixing_ref[...] = mixweights(
        bc_all[:, 0:state], bc_all[:, state : 2 * state], steps, params[0:8, 0:1], heads, tmp
    )
    loads[2].wait()
    arrived(first, INNER_K)
    scanned = apply_mix(mixing_ref[...], inner_all[...], params[0:8, 2:3], heads)
    loads[3].wait()
    arrived(first, GATE_K)
    gated = scanned * jax.nn.silu(gate_all[...].astype(F32))
    sq1_tx[...] = as_rows(jnp.sum(gated * gated, axis=1, keepdims=True))
    second = {}
    for d in order:
        second[SQ1_K, d] = send(SQ1_K, d, sq1_tx, sq1_rx.at[d])
    loads[11].wait()
    loads[12].wait()
    scaled = (gated * norm_gain[:, mine]).astype(BF)
    forward, total = exchange(OUT_K, scaled, out_w, out_tx, out_rx)
    for k in hops:
        forward(k)
    loads[4].wait()
    arrived(first, RES_K)
    arrived(second, SQ1_K)
    squares = sq1_tx[...]
    for d in order:
        squares = squares + sq1_rx[d]
    scale = as_column(lax.rsqrt(squares[0:1] / inner_width + 1e-05))
    hidden = (res_all[...].astype(F32) + scale * total()).astype(BF)
    to = lax.broadcasted_iota(jnp.int32, (rows, rows), 0)
    raster = lax.broadcasted_iota(jnp.int32, (rows, rows), 1)
    moved = (raster % peers) * (rows // peers) + raster // peers
    hidden = jnp.dot((to == moved).astype(BF), hidden, preferred_element_type=F32)

    width = in_w.shape[1]
    for load in loads[13:19]:
        load.wait()
    pre = (hidden * pre_gain[:, mine]).astype(BF)
    logits = lax.dot_general(
        step_weight[:, mine], pre, (((1,), (1,)), ((), ())), preferred_element_type=F32
    )
    squares = as_rows(jnp.sum(hidden * hidden, axis=1, keepdims=True))
    for p in range(peers):
        sq2_tx[p, 0:heads, :] = logits[p * heads : (p + 1) * heads]
        sq2_tx[p, heads:8, :] = squares[heads:8]
    third = {}
    for d in order:
        third[SQ2_K, d] = send(SQ2_K, d, sq2_tx.at[peer(d)], sq2_rx.at[d])
    proj_tx[...] = jnp.dot(
        pre, in_w[:, inner_width:width], preferred_element_type=F32
    ).astype(BF)
    for d in order:
        third[PROJ_K, d] = send(
            PROJ_K, d, proj_tx.at[at(peer(d), tok_rows), :], proj_rx.at[d]
        )

    forward, total = exchange(VAL_K, pre, in_w, val_tx, val_rx)
    for k in hops[:1]:
        forward(k)
    proj = proj_tx[my_rows, :].astype(F32)
    for d in order:
        third[PROJ_K, d].wait_recv()
        proj = proj + proj_rx[d].astype(F32)
    spread_tx[...] = proj.astype(BF)
    for d in order:
        third[SPREAD_K, d] = send(SPREAD_K, d, spread_tx, proj_all.at[my_rows, :])
    proj_all[my_rows, :] = spread_tx[...]
    for k in hops[1:]:
        forward(k)
    arrived(third, SQ2_K)
    gathered = sq2_tx[me]
    for d in order:
        gathered = gathered + sq2_rx[d]
    scale_row = lax.rsqrt(gathered[heads : heads + 1] / inner_width + 1e-05)
    scale = as_column(scale_row)
    steps = softplus(scale_row * gathered + params[0:8, 4:5])

    def bias_row(start, size):
        pieces = [conv_bias[pl.ds(start + i, 1), :] for i in range(size // 128)]
        return jnp.concatenate(pieces, axis=1)

    def convolve(projected, columns, bias):
        taps = conv_weight[:, columns].astype(F32)
        place = lax.broadcasted_iota(jnp.int32, projected.shape, 0)
        mixed = bias
        for offset in range(KC):
            back = KC - 1 - offset
            term = projected
            if back:
                term = jnp.where(place < back, 0.0, pltpu.roll(projected, back, 0))
            mixed = mixed + taps[offset : offset + 1] * term
        return jax.nn.silu(mixed).astype(BF)

    arrived(third, SPREAD_K)
    both = convolve(scale * proj_all[...].astype(F32), slice(inner_width, width), bias_row(inner_width // 128, width - inner_width))
    mixing_ref[...] = mixweights(
        both[:, 0:state], both[:, state : 2 * state], steps, params[0:8, 3:4], heads, tmp
    )
    values = convolve(scale * total(), mine, bias_row(me * (slab // 128), slab))
    scanned = apply_mix(mixing_ref[...], values, params[0:8, 5:6], heads).astype(BF)
    fin_tx[...] = scanned
    last = {}
    for d in order:
        last[FIN_K, d] = send(FIN_K, d, fin_tx.at[at(peer(d), tok_rows), :], fin.at[:, mine])
    fin[:, mine] = fin_tx[my_rows, :]
    arrived(last, FIN_K)
    result[...] = rms_scale(fin[...].astype(F32), final_gain[0]).astype(BF)
    for copy in flights:
        copy.wait_send()


def fused_local(peers, *args):
    (inner, gate, bc, raw, rate_one, bias_one, skip_one, norm_gain, out_w, residual) = args[:10]
    (pre_gain, in_w, conv_w, conv_bias, step_w, bias_two, rate_two, skip_two, final_gain) = args[10:]
    tok_rows, inner_width = inner.shape
    heads = rate_one.shape[0] // peers
    rows, slab = (tok_rows * peers, inner_width // peers)
    state2 = bc.shape[1]

    def flat(vector):
        return vector.reshape(1, vector.shape[0])

    big = (inner, gate, bc, raw, residual)
    small = tuple(map(flat, (rate_one, bias_one, skip_one, rate_two, bias_two, skip_two)))
    small += (out_w, flat(norm_gain), flat(pre_gain), in_w, step_w.T, conv_w)
    small += (conv_bias.reshape(-1, 128), flat(final_gain))
    block = pltpu.VMEM((rows, slab), BF)
    blocks = pltpu.VMEM((peers, rows, slab), BF)
    tiles = pltpu.VMEM((peers, 8, rows), F32)
    sends = pltpu.SemaphoreType.DMA((KINDS, peers))
    return pl.pallas_call(
        functools.partial(fused, peers, heads),
        out_shape=jax.ShapeDtypeStruct((tok_rows, inner_width), BF),
        in_specs=[pl.BlockSpec(memory_space=pltpu.HBM)] * (len(big) + len(small)),
        out_specs=pl.BlockSpec(memory_space=pltpu.VMEM),
        scratch_shapes=[pltpu.VMEM(part.shape, part.dtype) for part in small]
        + [
            block,
            block,
            pltpu.VMEM((rows, state2), BF),
            pltpu.VMEM((rows, raw.shape[1]), F32),
            block,
            blocks,
            blocks,
            pltpu.VMEM((8, rows), F32),
            tiles,
            blocks,
            blocks,
            pltpu.VMEM((rows, state2), BF),
            pltpu.VMEM((peers, tok_rows, state2), BF),
            pltpu.VMEM((tok_rows, state2), BF),
            pltpu.VMEM((rows, state2), BF),
            tiles,
            tiles,
            block,
            pltpu.VMEM((tok_rows, inner_width), BF),
            pltpu.VMEM((rows, rows), F32),
            pltpu.VMEM((heads * rows, rows), BF),
            pltpu.SemaphoreType.DMA((LOADS,)),
            sends,
            sends,
        ],
        compiler_params=pltpu.CompilerParams(
            collective_id=0, has_side_effects=True, vmem_limit_bytes=60 * 1024 * 1024
        ),
    )(*big, *small)


def local_step(peers, *args):
    inner, bc, rates = (args[0], args[2], args[4])
    tok_rows, inner_width = inner.shape
    heads = rates.shape[0]
    fits = (
        tok_rows * peers == 128
        and peers % 2 == 0
        and tok_rows % 16 == 0
        and tok_rows % peers == 0
        and heads % peers == 0
        and heads // peers < 8
        and heads <= 128
        and inner_width % (128 * peers) == 0
        and args[9].shape[1] == inner_width
        and bc.shape[1] == 256
    )
    return fused_local(peers, *args) if fits else local(*args)


def solution(mesh):
    placed = (
        P(("batch", "tok"), None),
        P(("batch", "tok"), None),
        P(("batch", "tok"), None),
        P(("batch", "tok"), None),
        P(),
        P(),
        P(),
        P(),
        P("tok", None),
        P(("batch", "tok"), None),
        P(),
        P("tok", None),
        P(),
        P(),
        P(),
        P(),
        P(),
        P(),
        P(),
    )
    return jax.shard_map(
        functools.partial(local_step, mesh.shape["tok"]), mesh=mesh, in_specs=placed, out_specs=P(("batch", "tok"), None), check_vma=False
    )
```
